32 devices in a mesh: depth: 16 (over z, y, x), slab: 2 (over core).
Axes of the slice: x: 2, y: 2, z: 4, core: 2. Of those that a mesh axis runs over, the one named last changes fastest.
Arguments:
- ref_feat: bfloat16 [4, 32, 128], P('slab'), may hold values from -9 to 9
- src_feat: bfloat16 [2560, 32, 128], P('depth'), may hold values from -9 to 9
- tile_owner: int32 [1280, 1], P(('depth', 'slab')), may hold values from 0 to 15; in each aligned block of 40 rows (0 to 39, 40 to 79, ...) at most 4 rows name the same one
- tile_local: int32 [1280], P(('depth', 'slab')), may hold values from 0 to 159
- col_shift: int32 [1280], P(('depth', 'slab')), may hold values from -16 to 16
- w_gates: bfloat16 [9, 64, 8], replicated, may hold values from -1.4375 to 1.4375
- bias_z: float32 [32], replicated
- bias_c: float32 [32], replicated, may hold values from -3 to 3
- w_out: float32 [32], replicated
Outputs:
- probability: float32 [64, 4, 128], P('depth', 'slab')
- depth_map: float32 [4, 128], P('slab')
The draws below stay inside these ranges and needn't reach their ends.
Inputs may be any that keep to these rules, and one draw needn't show every extreme that they name: `tile_owner`: among the requests of one device no owner is named more than 4 times; in some devices one owner is named exactly 4 times.
All inputs are finite; a program needn't handle non-finite values.
Results may differ from the reference program's by a relative error of at most 0.00085.
Values may be sent and summed in bfloat16 or wider, within the bound.
A program may use at most 64 MiB of HBM per device.

```python
import math
import jax
import jax.numpy as jnp
import numpy as np
from jax import lax

FEAT = 32
GROUPS = 8
HID = 32
VIEWS = 5
PD = 4
COLS = 128
MAXSHIFT = 16
RS = 2
SRC_DEV = 160
PLANES = 64
ROWS = 4
CPG = 4
REQ_DEV = 40
REQUESTS = 1280
CAP = 4
SRC_TILES = 2560
N_DEPTH = 16
N_SLAB = 2


def draw_bias_z(key, part):
    key_kind, key_slow, key_fast = jax.random.split(key, 3)
    kind_draw = jax.random.randint(key_kind, (HID,), 0, 2)
    slow_units = kind_draw < 1
    keep_rate = jax.random.uniform(key_slow, (HID,), jnp.float32, 0.3, 1.2)
    span_top = jnp.log(jnp.float32(max(PLANES / 4.0, 4.0)))
    span_log = jax.random.uniform(key_fast, (HID,), jnp.float32, 0.0, 1.0)
    fast_span = jnp.exp(jnp.log(jnp.float32(2.0)) + span_log * (span_top - jnp.log(jnp.float32(2.0))))
    log_retain = jnp.where(slow_units, -keep_rate / PLANES, -1.0 / fast_span)
    return (log_retain - jnp.log(-jnp.expm1(log_retain))).astype(jnp.float32)


def draw_w_out(key, part):
    return (jax.random.normal(key, (HID,), jnp.float32) * 3.0).astype(jnp.float32)


def set_ends(entries, rng, least, high):
    place = [jax.random.randint(jax.random.fold_in(rng, axis), (), 0, length) for axis, length in enumerate(entries.shape)]
    main_axis = entries.shape.index(max(entries.shape))
    neighbour = place[:main_axis] + [(place[main_axis] + 1) % entries.shape[main_axis]] + place[main_axis + 1:]
    return entries.at[tuple(place)].set(least).at[tuple(neighbour)].set(high)


def block_levels(own_key, extent, pieces, low, high):
    def one(dim, blocks):
        draws = jax.random.uniform(jax.random.fold_in(jax.random.fold_in(own_key, 6), dim), (blocks,), jnp.float32, low / len(pieces), high / len(pieces))
        return jnp.repeat(jnp.exp(draws), extent[dim] // blocks).reshape((-1,) + (1,) * (len(extent) - dim - 1))

    factor_of = one(*pieces[0])
    for cut in pieces[1:]:
        factor_of = factor_of * one(*cut)
    return factor_of


def shared_out(rng, own, number, rows, amount, top, reach, slope):
    order = jax.random.permutation(rng, amount)
    heavy_load, usual = load_shares(amount, rows * top, reach, slope, True), load_shares(amount, rows * top, reach, slope, False)
    places = jnp.arange(amount)

    def named(tallies, offset_by):
        used = int((tallies > 0).sum())
        fixed = max(1, used // 4)
        moved = fixed + (places - fixed + offset_by * (used - fixed)) % max(1, amount - fixed)
        return jnp.zeros((amount,), jnp.int32).at[order[jnp.where(places < fixed, places, moved)]].set(jnp.asarray(tallies, jnp.int32))

    tallies = jnp.where(number % 4 == 0, named(heavy_load, number // 4), named(usual, number - number // 4 - 1))
    mixed = jax.random.permutation(jax.random.fold_in(own, 3), amount)
    source_of, receiver = mixed[0:amount // 2 * 2:2], mixed[1:amount // 2 * 2:2]
    room = jnp.minimum(tallies[source_of] - 1, reach - tallies[receiver]) // 2
    room = jnp.where((source_of == order[0]) | (receiver == order[0]) | (tallies[receiver] == 0), 0, jnp.maximum(room, 0))
    moved = jax.random.randint(jax.random.fold_in(own, 4), (amount // 2,), 0, 1 << 20) % (room + 1)
    tallies = tallies.at[source_of].add(-moved).at[receiver].add(moved)
    members = jnp.searchsorted(jnp.cumsum(tallies), jnp.arange(rows * top), side="right").astype(jnp.int32)
    table = members.reshape(top, rows).T
    table = table[jax.random.permutation(jax.random.fold_in(own, 1), rows)]
    offset_by = jax.random.randint(jax.random.fold_in(own, 2), (rows, 1), 0, top)
    return jnp.take_along_axis(table, (jnp.arange(top)[None, :] + offset_by) % top, axis=1)


def load_shares(amount, total, bound, skew, full):
    weights = [(1 << 20) // math.isqrt(grade ** skew) + 1 for grade in range(1, amount + 1)]
    largest = bound if full else min(bound, max(-(-total // amount), total * weights[0] // sum(weights)))
    least = 1 if total - largest >= amount - 1 else 0
    given, spare = [largest] + [least] * (amount - 1), total - largest - least * (amount - 1)
    while spare > 0:
        movable = [i for i in range(1, amount) if given[i] < largest] or [i for i in range(1, amount) if given[i] < bound]
        whole, budget = sum([weights[i] for i in movable]), spare
        for i in movable:
            addition = min(bound - given[i], max(1, budget * weights[i] // whole), spare)
            given[i] = given[i] + addition
            spare = spare - addition
    return np.array(given)


def centred(rng, dims, spread, reach, shards=(), kind=jnp.bfloat16):
    result = jax.random.normal(rng, dims, jnp.float32) * spread
    if len(shards) > 0:
        result = block_levels(rng, dims, shards, -0.22, 0.18) * result
    return jnp.clip(result, min=-reach, max=reach).astype(kind)


def setup_inputs(seed: int = 0) -> dict:
    splits = jax.random.split(jax.random.key(seed), 10)
    ref_feat = centred(splits[0], (ROWS, FEAT, COLS), 1.5, 9.0, ((0, 2),))
    src_feat = centred(splits[1], (SRC_TILES, FEAT, COLS), 1.5, 9.0, ((0, 16),))
    tile_owner_keys = jax.random.split(jax.random.fold_in(splits[2], 1), REQUESTS // REQ_DEV)
    tile_owner_turns = jax.random.permutation(jax.random.fold_in(splits[2], 3), REQUESTS // REQ_DEV)
    tile_owner = jax.vmap(lambda own, number: shared_out(jax.random.fold_in(splits[2], 2), own, number, REQ_DEV, N_DEPTH, 1, CAP, 2))(tile_owner_keys, tile_owner_turns).reshape((REQUESTS, 1))
    tile_local = set_ends(jax.random.randint(splits[3], (REQUESTS,), 0, SRC_DEV), jax.random.fold_in(splits[3], 1), 0, SRC_DEV - 1).astype(jnp.int32)
    col_shift = set_ends(jax.random.randint(splits[4], (REQUESTS,), 0 - MAXSHIFT, MAXSHIFT + 1), jax.random.fold_in(splits[4], 1), 0 - MAXSHIFT, MAXSHIFT).astype(jnp.int32)
    w_gates = centred(splits[5], (9, 2 * HID, GROUPS), 0.24, 1.4375)
    bias_z = draw_bias_z(jax.random.fold_in(splits[9], 71), 0)
    bias_c = centred(splits[7], (HID,), 0.5, 3.0, (), jnp.float32)
    w_out = draw_w_out(jax.random.fold_in(splits[9], 71), 0)
    return {"ref_feat": ref_feat, "src_feat": src_feat, "tile_owner": tile_owner, "tile_local": tile_local, "col_shift": col_shift, "w_gates": w_gates, "bias_z": bias_z, "bias_c": bias_c, "w_out": w_out}


def arrange(values):
    shaped = values.reshape(N_DEPTH, N_SLAB, PD, VIEWS, RS)
    return shaped.transpose(0, 2, 3, 1, 4).reshape(PLANES, VIEWS, ROWS)


def reference(ref_feat, src_feat, tile_owner, tile_local, col_shift, w_gates, bias_z, bias_c, w_out):
    tile_all = arrange(tile_owner[:, 0].astype(jnp.int32) * SRC_DEV + tile_local.astype(jnp.int32))
    shift_all = arrange(col_shift.astype(jnp.int32))
    ref_wide = ref_feat.astype(jnp.float32)
    positions = jnp.arange(COLS, dtype=jnp.int32)
    gates_wide = w_gates.astype(jnp.float32)

    def plane_step(current, inputs):
        tile_ids, shift_now = inputs
        tile_rows = jnp.take(src_feat, tile_ids.reshape(-1), axis=0).reshape(VIEWS, ROWS, FEAT, COLS)
        source_col = positions[None, None, :] - shift_now[:, :, None]
        inside = (source_col >= 0) & (source_col < COLS)
        clipped = jnp.clip(source_col, 0, COLS - 1)
        index_full = jnp.broadcast_to(clipped[:, :, None, :], tile_rows.shape)
        moved = jnp.take_along_axis(tile_rows, index_full, axis=3)
        warped = jnp.where(inside[:, :, None, :], moved, jnp.zeros((), tile_rows.dtype))
        product = warped.astype(jnp.float32) * ref_wide[None]
        summed = product.reshape(VIEWS, ROWS, GROUPS, CPG, COLS).sum(axis=(0, 3))
        cost = summed / (VIEWS * CPG)
        padded = jnp.pad(cost, ((1, 1), (0, 0), (1, 1)))
        preact = jnp.zeros((ROWS, 2 * HID, COLS), jnp.float32)
        for tap_index in range(9):
            row_step = tap_index // 3
            col_step = tap_index % 3
            window = padded[row_step:row_step + ROWS, :, col_step:col_step + COLS]
            preact = preact + jnp.einsum("rgx,og->rox", window, gates_wide[tap_index], precision=lax.Precision.HIGHEST)
        retain = jax.nn.sigmoid(preact[:, :HID] + bias_z[None, :, None])
        candidate = jnp.tanh(preact[:, HID:] + bias_c[None, :, None])
        current = retain * current + (1.0 - retain) * candidate
        score = jnp.einsum("rox,o->rx", current, w_out, precision=lax.Precision.HIGHEST)
        return current, score

    start = jnp.zeros((ROWS, HID, COLS), jnp.float32)
    final_state, scores = lax.scan(plane_step, start, (tile_all, shift_all))
    highest = jnp.max(scores, axis=0)
    weights = jnp.exp(scores - highest[None])
    totals = jnp.sum(weights, axis=0)
    probability = weights / totals[None]
    plane_index = jnp.arange(PLANES, dtype=jnp.int32).astype(jnp.float32)
    depth_value = 1.0 / (0.1 + 0.9 * plane_index / (PLANES - 1))
    depth_map = jnp.sum(probability * depth_value[:, None, None], axis=0)
    return probability, depth_map
```

```python
import functools

import jax
import jax.numpy as jnp
from jax import lax
from jax.experimental import pallas as pl
from jax.experimental.pallas import tpu as pltpu
from jax.sharding import PartitionSpec as P

VIEWS = 5
PD = 4
MAXSHIFT = 16
MESH = pl.DeviceIdType.MESH
F32 = jnp.float32
I32 = jnp.int32


def kernel(
    n, cap, seg,
    ref_ref, src_hbm, owner_ref, local_ref, shift_ref, w_ref, bz_ref, bc_ref, wo_ref,
    prob_ref, depth_ref,
    src, ref_wide, tab_send, tab_recv, tab_s, own_v, own_s, prod, ans_send, ans_recv,
    edge_send, edge_recv, win, fwd_send, fwd_recv, back_send, back_recv, stat_send, stat_recv,
    src_sem, smem_sems, send_sems, recv_sems,
):
    me = lax.axis_index("depth")
    slab = lax.axis_index("slab")
    requests = owner_ref.shape[0]
    rows, feat, cols = ref_ref.shape
    groups = w_ref.shape[2]
    hidden = w_ref.shape[1] // 2
    cpg = feat // groups

    def peer(k):
        return lax.rem(me + k, n)

    barrier = pltpu.get_barrier_semaphore()

    def greet(k, carry):
        pl.semaphore_signal(barrier, inc=1, device_id={"depth": peer(k)}, device_id_type=MESH)
        return carry

    lax.fori_loop(1, n, greet, 0)
    pl.semaphore_signal(barrier, inc=1, device_id={"slab": 1 - slab}, device_id_type=MESH)
    src_copy = pltpu.make_async_copy(src_hbm, src, src_sem)
    src_copy.start()

    q_sub = lax.broadcasted_iota(I32, (requests, requests), 0)
    q_lane = lax.broadcasted_iota(I32, (requests, requests), 1)
    diag = q_sub == q_lane
    owner_col = owner_ref[...]
    owner_row = jnp.sum(jnp.where(diag, owner_col, 0), axis=0, keepdims=True)
    local_col = jnp.sum(jnp.where(diag, local_ref[...], 0).astype(F32), axis=1, keepdims=True)
    shift_col = jnp.sum(
        jnp.where(diag, shift_ref[...] + MAXSHIFT, 0).astype(F32), axis=1, keepdims=True
    )
    same = (owner_row == owner_col) & (q_lane < q_sub)
    slot_col = jnp.sum(jnp.where(same, 1.0, 0.0), axis=1, keepdims=True)
    lane = lax.broadcasted_iota(I32, (requests, cols), 1)
    row_col = lax.rem(lax.broadcasted_iota(I32, (requests, cols), 0), rows).astype(F32)
    kind = lane // cap
    value = jnp.where(
        kind == 0, local_col, jnp.where(kind == 1, shift_col, jnp.where(kind == 2, row_col, 0.0))
    )
    value = jnp.where(lax.rem(lane, cap).astype(F32) == slot_col, value, 0.0)
    owner_hot = jnp.where(
        lax.broadcasted_iota(I32, (n, requests), 0) == owner_row, 1.0, 0.0
    )
    table = jnp.dot(
        owner_hot.astype(jnp.bfloat16), value.astype(jnp.bfloat16), preferred_element_type=F32
    ).astype(I32)
    tab_send[:, 0, :] = table
    place_col = owner_col.astype(F32) * cap + slot_col
    wide_diag = lax.broadcasted_iota(I32, (requests, cols), 0) == lane
    own_v[...] = jnp.sum(jnp.where(wide_diag, place_col, 0.0), axis=0, keepdims=True).astype(I32)
    own_copy = pltpu.make_async_copy(own_v, own_s, smem_sems.at[0])
    own_copy.start()

    def push(source, target, who, number):
        return pltpu.make_async_remote_copy(
            src_ref=source, dst_ref=target, send_sem=send_sems.at[number],
            recv_sem=recv_sems.at[number], device_id=who, device_id_type=MESH,
        )

    def drain(buffer, number, sems):
        part = buffer.at[pl.ds(0, buffer.shape[0] // n * (n - 1))]
        pltpu.make_async_copy(part, part, sems.at[number]).wait()

    pl.semaphore_wait(barrier, n)

    def send_table(k, carry):
        to = peer(k)
        push(tab_send.at[to], tab_recv.at[me], {"depth": to}, 0).start()
        return carry

    lax.fori_loop(1, n, send_table, 0)
    tab_recv[me] = tab_send[me]
    ref_wide[...] = ref_ref[...].astype(F32)
    gates = jnp.concatenate([w_ref[t].astype(F32) for t in range(9)] * 2, axis=1)
    gates = gates.astype(jnp.bfloat16)
    h_eye = lax.broadcasted_iota(I32, (hidden, hidden), 0) == lax.broadcasted_iota(
        I32, (hidden, hidden), 1
    )

    def column(row):
        return jnp.sum(jnp.where(h_eye, row, 0.0), axis=1, keepdims=True)

    bias_z, bias_c, w_out = column(bz_ref[...]), column(bc_ref[...]), column(wo_ref[...])
    src_copy.wait()
    drain(tab_recv, 0, recv_sems)
    tab_copy = pltpu.make_async_copy(tab_recv, tab_s, smem_sems.at[1])
    tab_copy.start()
    tab_copy.wait()

    position = lax.broadcasted_iota(I32, (feat, cols), 1)

    def correlate(who, out, at):
        for s in range(cap):
            tile = jnp.clip(tab_s[who, 0, s], 0, src.shape[0] - 1)
            shift = jnp.clip(tab_s[who, 0, cap + s], 0, 2 * MAXSHIFT) - MAXSHIFT
            row = jnp.clip(tab_s[who, 0, 2 * cap + s], 0, rows - 1)
            wide = src[tile].astype(F32)
            moved = pltpu.roll(wide, lax.rem(shift + cols, cols), 1)
            source_col = position - shift
            inside = (source_col >= 0) & (source_col < cols)
            prod[s] = jnp.where(inside, moved, 0.0) * ref_wide[row]
            total = prod[s, pl.ds(0, groups, stride=cpg), :]
            for c in range(1, cpg):
                total = total + prod[s, pl.ds(c, groups, stride=cpg), :]
            out[at * cap + s] = total

    def answer(k, carry):
        to = peer(k)
        correlate(to, ans_send, to)
        push(
            ans_send.at[pl.ds(to * cap, cap)], ans_recv.at[pl.ds(me * cap, cap)], {"depth": to}, 1
        ).start()
        return carry

    lax.fori_loop(1, n, answer, 0)
    correlate(me, ans_recv, me)
    own_copy.wait()
    drain(ans_recv, 1, recv_sems)

    scale = 1.0 / (VIEWS * cpg)
    cost = {}
    for p in range(PD):
        for r in range(rows):
            total = None
            for v in range(VIEWS):
                place = jnp.clip(own_s[0, (p * VIEWS + v) * rows + r], 0, n * cap - 1)
                term = ans_recv[place]
                total = term if total is None else total + term
            cost[p, r] = total * scale
    for p in range(PD):
        edge_send[p] = jnp.where(slab == 0, cost[p, rows - 1], cost[p, 0])
    edge = push(edge_send, edge_recv, {"slab": 1 - slab}, 2)
    edge.start()

    glane = lax.broadcasted_iota(I32, (groups, cols), 1)
    half = 9 * groups

    def spread(p, r, x):
        for b in (-1, 0, 1):
            if b == -1:
                y = jnp.where(glane >= 1, pltpu.roll(x, 1, 1), 0.0)
            elif b == 1:
                y = jnp.where(glane < cols - 1, pltpu.roll(x, cols - 1, 1), 0.0)
            else:
                y = x
            high = y.astype(jnp.bfloat16).astype(F32)
            low = y - high
            for a in (-1, 0, 1):
                to = r - a
                if 0 <= to < rows:
                    t = (a + 1) * 3 + (b + 1)
                    at = pl.ds((p * rows + to) * cols, cols)
                    win[pl.ds(t * groups, groups), at] = high
                    win[pl.ds(half + t * groups, groups), at] = low

    for p in range(PD):
        for r in range(rows):
            spread(p, r, cost[p, r])
    edge.wait_recv()
    for p in range(PD):
        x = edge_recv[p]
        spread(p, -1, jnp.where(slab == 1, x, 0.0))
        spread(p, rows, jnp.where(slab == 0, x, 0.0))

    preact = jnp.dot(gates, win[...].astype(jnp.bfloat16), preferred_element_type=F32)
    retain = jax.nn.sigmoid(preact[:hidden] + bias_z)
    fresh = (1.0 - retain) * jnp.tanh(preact[hidden:] + bias_c)
    span = rows * cols
    decay, offset = [], []
    for p in range(PD):
        keep = retain[:, p * span : (p + 1) * span]
        new = fresh[:, p * span : (p + 1) * span]
        decay.append(keep if p == 0 else keep * decay[-1])
        offset.append(new if p == 0 else keep * offset[-1] + new)

    for r in range(rows):
        at = slice(r * cols, (r + 1) * cols)
        for j in range(hidden // seg):
            units = slice(j * seg, (j + 1) * seg)
            fwd_send[r * (hidden // seg) + j, 0:seg, :] = decay[-1][units, at]
            fwd_send[r * (hidden // seg) + j, seg : 2 * seg, :] = offset[-1][units, at]
    used = rows * hidden // seg
    if used < n:
        fwd_send[used:] = jnp.zeros((n - used, 2 * seg, cols), F32)

    def send_chunk(k, carry):
        to = peer(k)
        push(fwd_send.at[to], fwd_recv.at[me], {"depth": to}, 3).start()
        return carry

    lax.fori_loop(1, n, send_chunk, 0)
    fwd_recv[me] = fwd_send[me]
    decay_out = [w_out * x for x in decay]
    offset_out = [jnp.sum(w_out * x, axis=0, keepdims=True) for x in offset]
    drain(fwd_recv, 3, recv_sems)

    def compose(i, state):
        back_send[i] = state
        return fwd_recv[i, 0:seg, :] * state + fwd_recv[i, seg : 2 * seg, :]

    lax.fori_loop(0, n, compose, jnp.zeros((seg, cols), F32), unroll=n <= 16)

    def send_back(k, carry):
        to = peer(k)
        push(back_send.at[to], back_recv.at[me], {"depth": to}, 4).start()
        return carry

    lax.fori_loop(1, n, send_back, 0)
    back_recv[me] = back_send[me]
    drain(back_recv, 4, recv_sems)
    chunks = [back_recv[j] for j in range(used)]
    per_row = hidden // seg
    before = jnp.concatenate(
        [
            jnp.concatenate(chunks[r * per_row : (r + 1) * per_row], axis=0)
            for r in range(rows)
        ],
        axis=1,
    )

    scores = [
        jnp.sum(decay_out[p] * before, axis=0, keepdims=True) + offset_out[p] for p in range(PD)
    ]
    top = functools.reduce(jnp.maximum, scores)
    weights = [jnp.exp(s - top) for s in scores]
    total = functools.reduce(jnp.add, weights)
    values = []
    for p in range(PD):
        index = jnp.full((1, span), me * PD + p, I32).astype(F32)
        values.append(1.0 / (0.1 + 0.9 * index / (PD * n - 1)))
    weighted = functools.reduce(jnp.add, [w * v for w, v in zip(weights, values)])
    stat_send[0:1] = top
    stat_send[1:2] = total
    stat_send[2:3] = weighted

    def send_stat(k, carry):
        push(stat_send, stat_recv.at[me], {"depth": peer(k)}, 5).start()
        return carry

    lax.fori_loop(1, n, send_stat, 0)
    stat_recv[me] = stat_send[...]
    drain(stat_recv, 5, recv_sems)
    every = stat_recv[...]
    highest = jnp.max(every[:, 0:1, :], axis=0)
    share = jnp.exp(every[:, 0:1, :] - highest[None])
    totals = jnp.sum(share * every[:, 1:2, :], axis=0)
    depth_sum = jnp.sum(share * every[:, 2:3, :], axis=0)
    factor = jnp.exp(top - highest) / totals
    depth = depth_sum / totals
    for r in range(rows):
        at = slice(r * cols, (r + 1) * cols)
        depth_ref[r : r + 1, :] = depth[:, at]
        for p in range(PD):
            prob_ref[p, r : r + 1, :] = (weights[p] * factor)[:, at]

    drain(tab_send, 0, send_sems)
    drain(ans_send, 1, send_sems)
    edge.wait_send()
    drain(fwd_send, 3, send_sems)
    drain(back_send, 4, send_sems)
    drain(stat_recv, 5, send_sems)


def body(ref_feat, src_feat, tile_owner, tile_local, col_shift, w_gates, bias_z, bias_c, w_out):
    n = lax.axis_size("depth")
    rows, feat, cols = ref_feat.shape
    groups = w_gates.shape[2]
    hidden = w_gates.shape[1] // 2
    requests = tile_owner.shape[0]
    cap = max(2, (3 * requests + 2 * n - 1) // (2 * n))
    seg = max(1, rows * hidden // n)
    vmem = pl.BlockSpec(memory_space=pltpu.VMEM)
    return pl.pallas_call(
        functools.partial(kernel, n, cap, seg),
        out_shape=(
            jax.ShapeDtypeStruct((PD, rows, cols), F32),
            jax.ShapeDtypeStruct((rows, cols), F32),
        ),
        in_specs=[vmem, pl.BlockSpec(memory_space=pl.ANY)] + [vmem] * 7,
        out_specs=(vmem, vmem),
        scratch_shapes=[
            pltpu.VMEM(src_feat.shape, src_feat.dtype),
            pltpu.VMEM((rows, feat, cols), F32),
            pltpu.VMEM((n, 1, cols), I32),
            pltpu.VMEM((n, 1, cols), I32),
            pltpu.SMEM((n, 1, cols), I32),
            pltpu.VMEM((1, cols), I32),
            pltpu.SMEM((1, cols), I32),
            pltpu.VMEM((cap, feat, cols), F32),
            pltpu.VMEM((n * cap, groups, cols), F32),
            pltpu.VMEM((n * cap, groups, cols), F32),
            pltpu.VMEM((PD, groups, cols), F32),
            pltpu.VMEM((PD, groups, cols), F32),
            pltpu.VMEM((18 * groups, PD * rows * cols), F32),
            pltpu.VMEM((n, 2 * seg, cols), F32),
            pltpu.VMEM((n, 2 * seg, cols), F32),
            pltpu.VMEM((n, seg, cols), F32),
            pltpu.VMEM((n, seg, cols), F32),
            pltpu.VMEM((3, rows * cols), F32),
            pltpu.VMEM((n, 3, rows * cols), F32),
            pltpu.SemaphoreType.DMA,
            pltpu.SemaphoreType.DMA((2,)),
            pltpu.SemaphoreType.DMA((6,)),
            pltpu.SemaphoreType.DMA((6,)),
        ],
        compiler_params=pltpu.CompilerParams(
            collective_id=0, has_side_effects=True, vmem_limit_bytes=32 * 1024 * 1024
        ),
        cost_estimate=pl.CostEstimate(
            flops=2 * 144 * 64 * 1024, bytes_accessed=src_feat.size * 2, transcendentals=65536
        ),
    )(
        ref_feat, src_feat, tile_owner, tile_local.reshape(1, requests),
        col_shift.reshape(1, requests), w_gates, bias_z.reshape(1, hidden),
        bias_c.reshape(1, hidden), w_out.reshape(1, hidden),
    )


def solution(mesh):
    return jax.shard_map(
        body,
        mesh=mesh,
        in_specs=(
            P("slab", None, None),
            P("depth", None, None),
            P(("depth", "slab"), None),
            P(("depth", "slab")),
            P(("depth", "slab")),
            P(),
            P(),
            P(),
            P(),
        ),
        out_specs=(P("depth", "slab", None), P("slab", None)),
        check_vma=False,
    )
```

```python
import functools

import jax
import jax.numpy as jnp
from jax import lax
from jax.experimental import pallas as pl
from jax.experimental.pallas import tpu as pltpu
from jax.sharding import PartitionSpec as P

VIEWS = 5
PD = 4
MAXSHIFT = 16
MESH = pl.DeviceIdType.MESH
F32 = jnp.float32
I32 = jnp.int32


def kernel(
    n, cap, seg,
    ref_hbm, src_hbm, owner_hbm, local_hbm, shift_hbm, w_hbm, bz_hbm, bc_hbm, wo_hbm,
    prob_ref, depth_ref,
    ref_ref, src, owner_ref, local_ref, shift_ref, w_ref, bz_ref, bc_ref, wo_ref,
    src_wide, ref_wide, tab_send, tab_recv, tab_s, own_v, own_s, prod, ans_send, ans_recv,
    edge_send, edge_recv, win, edge_win, fwd_send, fwd_recv, back_send, back_recv, stat_send, stat_recv,
    in_sems, smem_sems, send_sems, recv_sems,
):
    me = lax.axis_index("depth")
    slab = lax.axis_index("slab")
    requests = owner_ref.shape[1]
    rows, feat, cols = ref_ref.shape
    groups = w_ref.shape[1]
    hidden = w_ref.shape[2] // 2
    cpg = feat // groups

    def peer(k):
        return lax.rem(me + k, n)

    pairs = [
        (owner_hbm, owner_ref), (local_hbm, local_ref), (shift_hbm, shift_ref), (ref_hbm, ref_ref),
        (src_hbm, src), (w_hbm, w_ref), (bz_hbm, bz_ref), (bc_hbm, bc_ref), (wo_hbm, wo_ref),
    ]
    loads = [pltpu.make_async_copy(a, b, in_sems.at[i]) for i, (a, b) in enumerate(pairs)]
    for load in loads:
        load.start()
    barrier = pltpu.get_barrier_semaphore()

    def greet(k, carry):
        pl.semaphore_signal(barrier, inc=1, device_id={"depth": peer(k)}, device_id_type=MESH)
        return carry

    lax.fori_loop(1, n, greet, 0)
    pl.semaphore_signal(barrier, inc=1, device_id={"slab": 1 - slab}, device_id_type=MESH)

    q_sub = lax.broadcasted_iota(I32, (requests, requests), 0)
    q_lane = lax.broadcasted_iota(I32, (requests, requests), 1)
    diag = q_sub == q_lane
    for load in loads[:3]:
        load.wait()
    owner_row = owner_ref[...]
    owner_col = jnp.sum(
        jnp.where(diag, owner_row, 0).astype(F32), axis=1, keepdims=True
    ).astype(I32)
    local_col = jnp.sum(jnp.where(diag, local_ref[...], 0).astype(F32), axis=1, keepdims=True)
    shift_col = jnp.sum(
        jnp.where(diag, shift_ref[...] + MAXSHIFT, 0).astype(F32), axis=1, keepdims=True
    )
    same = (owner_row == owner_col) & (q_lane < q_sub)
    slot_col = jnp.sum(jnp.where(same, 1.0, 0.0), axis=1, keepdims=True)
    lane = lax.broadcasted_iota(I32, (requests, cols), 1)
    row_col = lax.rem(lax.broadcasted_iota(I32, (requests, cols), 0), rows).astype(F32)
    kind = lane // cap
    value = jnp.where(
        kind == 0, local_col, jnp.where(kind == 1, shift_col, jnp.where(kind == 2, row_col, 0.0))
    )
    value = jnp.where(lax.rem(lane, cap).astype(F32) == slot_col, value, 0.0)
    owner_hot = jnp.where(
        lax.broadcasted_iota(I32, (n, requests), 0) == owner_row, 1.0, 0.0
    )
    table = jnp.dot(
        owner_hot.astype(jnp.bfloat16), value.astype(jnp.bfloat16), preferred_element_type=F32
    ).astype(I32)
    tab_send[:, 0, :] = table
    place_col = owner_col.astype(F32) * cap + slot_col
    wide_diag = lax.broadcasted_iota(I32, (requests, cols), 0) == lane
    own_v[...] = jnp.sum(jnp.where(wide_diag, place_col, 0.0), axis=0, keepdims=True).astype(I32)
    own_copy = pltpu.make_async_copy(own_v, own_s, smem_sems.at[0])
    own_copy.start()

    def push(source, target, who, number):
        return pltpu.make_async_remote_copy(
            src_ref=source, dst_ref=target, send_sem=send_sems.at[number],
            recv_sem=recv_sems.at[number], device_id=who, device_id_type=MESH,
        )

    def drain(buffer, number, sems):
        part = buffer.at[pl.ds(0, buffer.shape[0] // n * (n - 1))]
        pltpu.make_async_copy(part, part, sems.at[number]).wait()

    pl.semaphore_wait(barrier, n)

    def send_table(k, carry):
        to = peer(k)
        push(tab_send.at[to], tab_recv.at[me], {"depth": to}, 0).start()
        return carry

    lax.fori_loop(1, n, send_table, 0)
    tab_recv[me] = tab_send[me]
    for load in loads[3:]:
        load.wait()

    def regroup(source, target, count, step):
        def some(i, carry):
            for j in range(step):
                prod[j] = source[i * step + j].astype(F32)
            for j in range(step):
                for c in range(cpg):
                    part = prod[j, pl.ds(c, groups, stride=cpg), :]
                    target[i * step + j, pl.ds(c * groups, groups), :] = part
            return carry

        lax.fori_loop(0, count // step, some, 0)

    regroup(ref_ref, ref_wide, rows, rows)
    regroup(src, src_wide, src.shape[0], 8)
    gates_t = w_ref[...].astype(F32).reshape(9 * groups, 2 * hidden)
    gates_t = jnp.concatenate([gates_t, jnp.zeros((128 - 9 * groups, 2 * hidden), F32)], axis=0)
    gates_1 = jnp.transpose(gates_t)[:, : 9 * groups]
    gates = jnp.concatenate([gates_1, gates_1], axis=1).astype(jnp.bfloat16)
    side = 3 * groups
    edge_1 = jnp.where(slab == 0, gates_1[:, 2 * side :], gates_1[:, :side])
    edge_gates = jnp.concatenate([edge_1, edge_1], axis=1).astype(jnp.bfloat16)
    h_eye = lax.broadcasted_iota(I32, (hidden, hidden), 0) == lax.broadcasted_iota(
        I32, (hidden, hidden), 1
    )

    def column(row):
        return jnp.sum(jnp.where(h_eye, row, 0.0), axis=1, keepdims=True)

    bias_z, bias_c, w_out = column(bz_ref[...]), column(bc_ref[...]), column(wo_ref[...])
    half = 9 * groups
    for at in (0, half):
        for p in range(PD):
            for r, a in ((0, 0), (rows - 1, 2)):
                win[pl.ds(at + a * side, side), pl.ds((p * rows + r) * cols, cols)] = jnp.zeros(
                    (side, cols), F32
                )
    drain(tab_recv, 0, recv_sems)
    tab_copy = pltpu.make_async_copy(tab_recv, tab_s, smem_sems.at[1])
    tab_copy.start()
    tab_copy.wait()

    position = lax.broadcasted_iota(I32, (groups, cols), 1)

    def correlate(who, out, at):
        tiles, shifts, picked = [], [], []
        for s in range(cap):
            tiles.append(jnp.clip(tab_s[who, 0, s], 0, src.shape[0] - 1))
            shifts.append(jnp.clip(tab_s[who, 0, cap + s], 0, 2 * MAXSHIFT) - MAXSHIFT)
            picked.append(jnp.clip(tab_s[who, 0, 2 * cap + s], 0, rows - 1))
        moved = [
            pltpu.roll(src_wide[tiles[s]], lax.rem(shifts[s] + cols, cols), 1) for s in range(cap)
        ]
        for s in range(cap):
            terms = moved[s] * ref_wide[picked[s]]
            total = terms[0:groups]
            for c in range(1, cpg):
                total = total + terms[c * groups : (c + 1) * groups]
            source_col = position - shifts[s]
            inside = (source_col >= 0) & (source_col < cols)
            out[at * cap + s] = jnp.where(inside, total, 0.0)

    def answer(k, carry):
        to = peer(k)
        correlate(to, ans_send, to)
        push(
            ans_send.at[pl.ds(to * cap, cap)], ans_recv.at[pl.ds(me * cap, cap)], {"depth": to}, 1
        ).start()
        return carry

    lax.fori_loop(1, n, answer, 0)
    correlate(me, ans_recv, me)
    own_copy.wait()
    drain(ans_recv, 1, recv_sems)

    scale = 1.0 / (VIEWS * cpg)
    cost = {}
    for p in range(PD):
        for r in range(rows):
            total = None
            for v in range(VIEWS):
                place = jnp.clip(own_s[0, (p * VIEWS + v) * rows + r], 0, n * cap - 1)
                term = ans_recv[place]
                total = term if total is None else total + term
            cost[p, r] = total * scale
    for p in range(PD):
        edge_send[p] = jnp.where(slab == 0, cost[p, rows - 1], cost[p, 0])
    edge = push(edge_send, edge_recv, {"slab": 1 - slab}, 2)
    edge.start()

    def turns(x):
        ahead = jnp.where(position >= 1, pltpu.roll(x, 1, 1), 0.0)
        behind = jnp.where(position < cols - 1, pltpu.roll(x, cols - 1, 1), 0.0)
        for b, y in enumerate((ahead, x, behind)):
            high = y.astype(jnp.bfloat16).astype(F32)
            yield b, high, y - high

    for p in range(PD):
        for r in range(rows):
            for b, high, low in turns(cost[p, r]):
                for a in (-1, 0, 1):
                    if 0 <= r - a < rows:
                        t = (a + 1) * 3 + b
                        at = pl.ds((p * rows + r - a) * cols, cols)
                        win[pl.ds(t * groups, groups), at] = high
                        win[pl.ds(half + t * groups, groups), at] = low
    inner = jnp.dot(gates, win[...].astype(jnp.bfloat16), preferred_element_type=F32)
    edge.wait_recv()
    for p in range(PD):
        for b, high, low in turns(edge_recv[p]):
            edge_win[pl.ds(b * groups, groups), pl.ds(p * cols, cols)] = high
            edge_win[pl.ds(side + b * groups, groups), pl.ds(p * cols, cols)] = low
    outer = jnp.dot(edge_gates, edge_win[...].astype(jnp.bfloat16), preferred_element_type=F32)
    pieces = []
    for p in range(PD):
        beside = outer[:, p * cols : (p + 1) * cols]
        for r in range(rows):
            piece = inner[:, (p * rows + r) * cols : (p * rows + r + 1) * cols]
            if r == 0:
                piece = piece + jnp.where(slab == 1, beside, 0.0)
            if r == rows - 1:
                piece = piece + jnp.where(slab == 0, beside, 0.0)
            pieces.append(piece)
    preact = jnp.concatenate(pieces, axis=1)
    retain = jax.nn.sigmoid(preact[:hidden] + bias_z)
    fresh = (1.0 - retain) * jnp.tanh(preact[hidden:] + bias_c)
    span = rows * cols
    decay, offset = [], []
    for p in range(PD):
        keep = retain[:, p * span : (p + 1) * span]
        new = fresh[:, p * span : (p + 1) * span]
        decay.append(keep if p == 0 else keep * decay[-1])
        offset.append(new if p == 0 else keep * offset[-1] + new)

    for r in range(rows):
        at = slice(r * cols, (r + 1) * cols)
        for j in range(hidden // seg):
            units = slice(j * seg, (j + 1) * seg)
            fwd_send[r * (hidden // seg) + j, 0:seg, :] = decay[-1][units, at]
            fwd_send[r * (hidden // seg) + j, seg : 2 * seg, :] = offset[-1][units, at]
    used = rows * hidden // seg
    if used < n:
        fwd_send[used:] = jnp.zeros((n - used, 2 * seg, cols), F32)

    def send_chunk(k, carry):
        to = peer(k)
        push(fwd_send.at[to], fwd_recv.at[me], {"depth": to}, 3).start()
        return carry

    lax.fori_loop(1, n, send_chunk, 0)
    fwd_recv[me] = fwd_send[me]
    decay_out = [w_out * x for x in decay]
    offset_out = [jnp.sum(w_out * x, axis=0, keepdims=True) for x in offset]
    drain(fwd_recv, 3, recv_sems)

    def compose(i, state):
        back_send[i] = state
        return fwd_recv[i, 0:seg, :] * state + fwd_recv[i, seg : 2 * seg, :]

    lax.fori_loop(0, n, compose, jnp.zeros((seg, cols), F32), unroll=n <= 16)

    def send_back(k, carry):
        to = peer(k)
        push(back_send.at[to], back_recv.at[me], {"depth": to}, 4).start()
        return carry

    lax.fori_loop(1, n, send_back, 0)
    back_recv[me] = back_send[me]
    drain(back_recv, 4, recv_sems)
    chunks = [back_recv[j] for j in range(used)]
    per_row = hidden // seg
    before = jnp.concatenate(
        [
            jnp.concatenate(chunks[r * per_row : (r + 1) * per_row], axis=0)
            for r in range(rows)
        ],
        axis=1,
    )

    scores = [
        jnp.sum(decay_out[p] * before, axis=0, keepdims=True) + offset_out[p] for p in range(PD)
    ]
    top = functools.reduce(jnp.maximum, scores)
    weights = [jnp.exp(s - top) for s in scores]
    total = functools.reduce(jnp.add, weights)
    values = []
    for p in range(PD):
        index = jnp.full((1, span), me * PD + p, I32).astype(F32)
        values.append(1.0 / (0.1 + 0.9 * index / (PD * n - 1)))
    weighted = functools.reduce(jnp.add, [w * v for w, v in zip(weights, values)])
    stat_send[0:1] = top
    stat_send[1:2] = total
    stat_send[2:3] = weighted

    def send_stat(k, carry):
        push(stat_send, stat_recv.at[me], {"depth": peer(k)}, 5).start()
        return carry

    lax.fori_loop(1, n, send_stat, 0)
    stat_recv[me] = stat_send[...]
    drain(stat_recv, 5, recv_sems)
    every = stat_recv[...]
    highest = jnp.max(every[:, 0:1, :], axis=0)
    share = jnp.exp(every[:, 0:1, :] - highest[None])
    totals = jnp.sum(share * every[:, 1:2, :], axis=0)
    depth_sum = jnp.sum(share * every[:, 2:3, :], axis=0)
    factor = jnp.exp(top - highest) / totals
    depth = depth_sum / totals
    for r in range(rows):
        at = slice(r * cols, (r + 1) * cols)
        depth_ref[r : r + 1, :] = depth[:, at]
        for p in range(PD):
            prob_ref[p, r : r + 1, :] = (weights[p] * factor)[:, at]

    drain(tab_send, 0, send_sems)
    drain(ans_send, 1, send_sems)
    edge.wait_send()
    drain(fwd_send, 3, send_sems)
    drain(back_send, 4, send_sems)
    drain(stat_recv, 5, send_sems)


def body(ref_feat, src_feat, tile_owner, tile_local, col_shift, w_gates, bias_z, bias_c, w_out):
    n = lax.axis_size("depth")
    rows, feat, cols = ref_feat.shape
    groups = w_gates.shape[2]
    hidden = w_gates.shape[1] // 2
    requests = tile_owner.shape[0]
    cap = max(2, (3 * requests + 2 * n - 1) // (2 * n))
    seg = max(1, rows * hidden // n)
    vmem = pl.BlockSpec(memory_space=pltpu.VMEM)
    return pl.pallas_call(
        functools.partial(kernel, n, cap, seg),
        out_shape=(
            jax.ShapeDtypeStruct((PD, rows, cols), F32),
            jax.ShapeDtypeStruct((rows, cols), F32),
        ),
        in_specs=[pl.BlockSpec(memory_space=pl.ANY)] * 9,
        out_specs=(vmem, vmem),
        scratch_shapes=[
            pltpu.VMEM(ref_feat.shape, ref_feat.dtype),
            pltpu.VMEM(src_feat.shape, src_feat.dtype),
            pltpu.VMEM((1, requests), I32),
            pltpu.VMEM((1, requests), I32),
            pltpu.VMEM((1, requests), I32),
            pltpu.VMEM((9, groups, 2 * hidden), w_gates.dtype),
            pltpu.VMEM((1, hidden), F32),
            pltpu.VMEM((1, hidden), F32),
            pltpu.VMEM((1, hidden), F32),
            pltpu.VMEM(src_feat.shape, F32),
            pltpu.VMEM(ref_feat.shape, F32),
            pltpu.VMEM((n, 1, cols), I32),
            pltpu.VMEM((n, 1, cols), I32),
            pltpu.SMEM((n, 1, cols), I32),
            pltpu.VMEM((1, cols), I32),
            pltpu.SMEM((1, cols), I32),
            pltpu.VMEM((8, feat, cols), F32),
            pltpu.VMEM((n * cap, groups, cols), F32),
            pltpu.VMEM((n * cap, groups, cols), F32),
            pltpu.VMEM((PD, groups, cols), F32),
            pltpu.VMEM((PD, groups, cols), F32),
            pltpu.VMEM((18 * groups, PD * rows * cols), F32),
            pltpu.VMEM((6 * groups, PD * cols), F32),
            pltpu.VMEM((n, 2 * seg, cols), F32),
            pltpu.VMEM((n, 2 * seg, cols), F32),
            pltpu.VMEM((n, seg, cols), F32),
            pltpu.VMEM((n, seg, cols), F32),
            pltpu.VMEM((3, rows * cols), F32),
            pltpu.VMEM((n, 3, rows * cols), F32),
            pltpu.SemaphoreType.DMA((9,)),
            pltpu.SemaphoreType.DMA((2,)),
            pltpu.SemaphoreType.DMA((6,)),
            pltpu.SemaphoreType.DMA((6,)),
        ],
        compiler_params=pltpu.CompilerParams(
            collective_id=0, has_side_effects=True, vmem_limit_bytes=60 * 1024 * 1024
        ),
        cost_estimate=pl.CostEstimate(
            flops=2 * 144 * 64 * 1024, bytes_accessed=src_feat.size * 2, transcendentals=65536
        ),
    )(
        ref_feat, src_feat, tile_owner.reshape(1, requests), tile_local.reshape(1, requests),
        col_shift.reshape(1, requests), jnp.transpose(w_gates, (0, 2, 1)), bias_z.reshape(1, hidden),
        bias_c.reshape(1, hidden), w_out.reshape(1, hidden),
    )


def solution(mesh):
    return jax.shard_map(
        body,
        mesh=mesh,
        in_specs=(
            P("slab", None, None),
            P("depth", None, None),
            P(("depth", "slab"), None),
            P(("depth", "slab")),
            P(("depth", "slab")),
            P(),
            P(),
            P(),
            P(),
        ),
        out_specs=(P("depth", "slab", None), P("slab", None)),
        check_vma=False,
    )
```

```python
import functools

import jax
import jax.numpy as jnp
from jax import lax
from jax.experimental import pallas as pl
from jax.experimental.pallas import tpu as pltpu
from jax.sharding import PartitionSpec as P

VIEWS = 5
PD = 4
MAXSHIFT = 16
MESH = pl.DeviceIdType.MESH
F32 = jnp.float32
I32 = jnp.int32


def kernel(
    n, cap,
    ref_hbm, src_hbm, owner_hbm, local_hbm, shift_hbm, w_hbm, bz_hbm, bc_hbm, wo_hbm,
    prob_ref, depth_ref,
    ref_ref, src, owner_ref, local_ref, shift_ref, w_ref, bz_ref, bc_ref, wo_ref,
    src_wide, ref_wide, tab_send, tab_recv, tab_s, own_v, own_s, prod, ans_send, ans_recv,
    gates_wide, gates, own_send, own_recv, side_send, side_recv, entry, fin_send, fin_recv,
    in_sems, smem_sems, send_sems, recv_sems,
):
    me = lax.axis_index("depth")
    slab = lax.axis_index("slab")
    requests = owner_ref.shape[1]
    rows, feat, cols = ref_ref.shape
    groups = w_ref.shape[1]
    hidden = w_ref.shape[2] // 2
    cpg = feat // groups

    edge = 8
    holders = cols // edge
    once = n <= 16

    def peer(k):
        return lax.rem(me + k, n)

    def far(j):
        step = (j + 1) // 2
        return peer(n // 2 + jnp.where(lax.rem(j, 2) == 1, -step, step))

    pairs = [
        (owner_hbm, owner_ref), (local_hbm, local_ref), (shift_hbm, shift_ref), (ref_hbm, ref_ref),
        (src_hbm, src), (w_hbm, w_ref), (bz_hbm, bz_ref), (bc_hbm, bc_ref), (wo_hbm, wo_ref),
    ]
    loads = [pltpu.make_async_copy(a, b, in_sems.at[i]) for i, (a, b) in enumerate(pairs)]
    for load in loads:
        load.start()
    barrier = pltpu.get_barrier_semaphore()

    def greet(k, carry):
        pl.semaphore_signal(barrier, inc=1, device_id={"depth": peer(k)}, device_id_type=MESH)
        return carry

    def greet_side(k, carry):
        who = {"depth": peer(k), "slab": 1 - slab}
        pl.semaphore_signal(barrier, inc=1, device_id=who, device_id_type=MESH)
        return carry

    lax.fori_loop(1, n, greet, 0, unroll=once)
    lax.fori_loop(0, n, greet_side, 0, unroll=once)

    q_sub = lax.broadcasted_iota(I32, (requests, requests), 0)
    q_lane = lax.broadcasted_iota(I32, (requests, requests), 1)
    diag = q_sub == q_lane
    for load in loads[:3]:
        load.wait()
    owner_row = owner_ref[...]
    owner_col = jnp.sum(
        jnp.where(diag, owner_row, 0).astype(F32), axis=1, keepdims=True
    ).astype(I32)
    local_col = jnp.sum(jnp.where(diag, local_ref[...], 0).astype(F32), axis=1, keepdims=True)
    shift_col = jnp.sum(
        jnp.where(diag, shift_ref[...] + MAXSHIFT, 0).astype(F32), axis=1, keepdims=True
    )
    same = (owner_row == owner_col) & (q_lane < q_sub)
    slot_col = jnp.sum(jnp.where(same, 1.0, 0.0), axis=1, keepdims=True)
    lane = lax.broadcasted_iota(I32, (requests, cols), 1)
    row_col = lax.rem(lax.broadcasted_iota(I32, (requests, cols), 0), rows).astype(F32)
    kind = lane // cap
    value = jnp.where(
        kind == 0, local_col, jnp.where(kind == 1, shift_col, jnp.where(kind == 2, row_col, 0.0))
    )
    value = jnp.where(lax.rem(lane, cap).astype(F32) == slot_col, value, 0.0)
    owner_hot = jnp.where(
        lax.broadcasted_iota(I32, (n, requests), 0) == owner_row, 1.0, 0.0
    )
    table = jnp.dot(
        owner_hot.astype(jnp.bfloat16), value.astype(jnp.bfloat16), preferred_element_type=F32
    ).astype(I32)
    tab_send[:, 0, :] = table
    place_col = owner_col.astype(F32) * cap + slot_col
    wide_diag = lax.broadcasted_iota(I32, (requests, cols), 0) == lane
    own_v[...] = jnp.sum(jnp.where(wide_diag, place_col, 0.0), axis=0, keepdims=True).astype(I32)
    own_copy = pltpu.make_async_copy(own_v, own_s, smem_sems.at[0])
    own_copy.start()

    def push(source, target, who, number):
        return pltpu.make_async_remote_copy(
            src_ref=source, dst_ref=target, send_sem=send_sems.at[number],
            recv_sem=recv_sems.at[number], device_id=who, device_id_type=MESH,
        )

    def drain(buffer, count, number, sems):
        part = buffer.at[pl.ds(0, count)]
        pltpu.make_async_copy(part, part, sems.at[number]).wait()

    pl.semaphore_wait(barrier, 2 * n - 1)

    def send_table(k, carry):
        to = far(k)
        push(tab_send.at[to], tab_recv.at[me], {"depth": to}, 0).start()
        return carry

    lax.fori_loop(0, n - 1, send_table, 0, unroll=once)
    tab_recv[me] = tab_send[me]
    for load in loads[3:]:
        load.wait()

    def regroup(source, target, count, step):
        def some(i, carry):
            for j in range(step):
                prod[j] = source[i * step + j].astype(F32)
            for j in range(step):
                for c in range(cpg):
                    part = prod[j, pl.ds(c, groups, stride=cpg), :]
                    target[i * step + j, pl.ds(c * groups, groups), :] = part
            return carry

        lax.fori_loop(0, count // step, some, 0)

    regroup(ref_ref, ref_wide, rows, rows)
    regroup(src, src_wide, src.shape[0], 8)
    taps = [w_ref[t].astype(F32) for t in range(9)]
    span = PD * rows * hidden
    plane_of = lax.broadcasted_iota(I32, (groups, span), 1) // (rows * hidden)

    def fill(at, pieces):
        for kind in range(2):
            units = slice(kind * hidden, (kind + 1) * hidden)
            part = jnp.concatenate([x[:, units] for x in pieces] * PD, axis=1)
            for p in range(PD):
                gates_wide[pl.ds(at(p), groups), pl.ds(kind * span, span)] = jnp.where(
                    plane_of == p, part, 0.0
                )

    own_rows = PD * rows * groups
    for b in range(3):
        for r in range(rows):
            fill(
                lambda p: b * cols + (p * rows + r) * groups,
                [taps[(r - to + 1) * 3 + b] for to in range(rows)],
            )
        pieces = [jnp.zeros((groups, 2 * hidden), F32) for _ in range(rows)]
        pieces[0] = pieces[0] + jnp.where(slab == 1, taps[b], 0.0)
        pieces[-1] = pieces[-1] + jnp.where(slab == 0, taps[6 + b], 0.0)
        fill(lambda p: b * cols + own_rows + p * groups, pieces)
        rest = own_rows + PD * groups
        gates_wide[pl.ds(b * cols + rest, cols - rest), :] = jnp.zeros((cols - rest, 2 * span), F32)
    gates[...] = gates_wide[...].astype(jnp.bfloat16)
    bias_z = jnp.concatenate([bz_ref[...]] * (PD * rows), axis=1)
    bias_c = jnp.concatenate([bc_ref[...]] * (PD * rows), axis=1)
    h_eye = lax.broadcasted_iota(I32, (hidden, hidden), 0) == lax.broadcasted_iota(
        I32, (hidden, hidden), 1
    )
    out_col = jnp.sum(jnp.where(h_eye, wo_ref[...], 0.0), axis=1, keepdims=True)
    out_col = jnp.concatenate([out_col] * (PD * rows), axis=0)
    unit_block = lax.broadcasted_iota(I32, (span, cols), 0) // hidden
    lane_block = lax.rem(lax.broadcasted_iota(I32, (span, cols), 1), PD * rows)
    out_wide = jnp.where(unit_block == lane_block, out_col, 0.0)
    out_high = out_wide.astype(jnp.bfloat16)
    out_low = (out_wide - out_high.astype(F32)).astype(jnp.bfloat16)
    drain(tab_recv, n - 1, 0, recv_sems)
    tab_copy = pltpu.make_async_copy(tab_recv, tab_s, smem_sems.at[1])
    tab_copy.start()
    tab_copy.wait()

    position = lax.broadcasted_iota(I32, (groups, cols), 1)

    def correlate(who, out, at):
        tiles, shifts, picked = [], [], []
        for s in range(cap):
            tiles.append(jnp.clip(tab_s[who, 0, s], 0, src.shape[0] - 1))
            shifts.append(jnp.clip(tab_s[who, 0, cap + s], 0, 2 * MAXSHIFT) - MAXSHIFT)
            picked.append(jnp.clip(tab_s[who, 0, 2 * cap + s], 0, rows - 1))
        moved = [
            pltpu.roll(src_wide[tiles[s]], lax.rem(shifts[s] + cols, cols), 1) for s in range(cap)
        ]
        for s in range(cap):
            terms = moved[s] * ref_wide[picked[s]]
            total = terms[0:groups]
            for c in range(1, cpg):
                total = total + terms[c * groups : (c + 1) * groups]
            source_col = position - shifts[s]
            inside = (source_col >= 0) & (source_col < cols)
            out[at * cap + s] = jnp.where(inside, total, 0.0)

    def answer(k, carry):
        to = far(k)
        correlate(to, ans_send, to)
        push(
            ans_send.at[pl.ds(to * cap, cap)], ans_recv.at[pl.ds(me * cap, cap)], {"depth": to}, 1
        ).start()
        return carry

    lax.fori_loop(0, n - 1, answer, 0)
    correlate(me, ans_recv, me)
    own_copy.wait()
    drain(ans_recv, cap * (n - 1), 1, recv_sems)

    scale = 1.0 / (VIEWS * cpg)
    cost = {}
    for p in range(PD):
        for r in range(rows):
            total = None
            for v in range(VIEWS):
                place = jnp.clip(own_s[0, (p * VIEWS + v) * rows + r], 0, n * cap - 1)
                term = ans_recv[place]
                total = term if total is None else total + term
            cost[p, r] = total * scale

    in_block = lax.rem(position, edge)

    def rim(x):
        left = jnp.where(position == 0, 0.0, pltpu.roll(x, 1, 1))
        right = jnp.where(position == cols - 1, 0.0, pltpu.roll(x, cols - 1, 1))
        return jnp.where(in_block == 0, left, right)

    blocks = [cost[p, r] for p in range(PD) for r in range(rows)]
    near = [jnp.where(slab == 0, cost[p, rows - 1], cost[p, 0]) for p in range(PD)]
    gap = jnp.zeros((cols // 2 - PD * groups, cols), F32)
    side = jnp.concatenate([rim(x) for x in near] + [gap] + near + [gap], axis=0)
    side_send[...] = jnp.transpose(side).reshape(holders, edge, cols)

    def send_side(k, carry):
        to = far(k) if n == holders else k
        who = {"depth": to, "slab": 1 - slab}
        push(side_send.at[to], side_recv.at[me], who, 3).start()
        return carry

    own = jnp.concatenate(blocks + [rim(x) for x in blocks], axis=0)
    own_send[...] = jnp.transpose(own).reshape(holders, edge, cols)

    def send_own(k, carry):
        to = far(k) if n == holders else k

        def go():
            push(own_send.at[to], own_recv.at[me], {"depth": to}, 2).start()

        go() if n == holders else pl.when(to != me)(go)
        return carry

    if n == holders:
        def send_both(k, carry):
            send_own(k, carry)
            return send_side(k, carry)

        lax.fori_loop(0, n - 1, send_both, 0, unroll=once)
        push(side_send.at[me], side_recv.at[me], {"depth": me, "slab": 1 - slab}, 3).start()
    else:
        lax.fori_loop(0, holders, send_own, 0)
        lax.fori_loop(0, holders, send_side, 0)

    def hold():
        own_recv[me] = own_send[me]
        drain(own_recv, n - 1, 2, recv_sems)
        drain(side_recv, n, 3, recv_sems)
        count = n * edge
        here = own_recv[...].reshape(count, cols)
        beside = side_recv[...].reshape(count, cols)
        lane = lax.broadcasted_iota(I32, (count, cols), 1)
        place = lax.rem(lax.broadcasted_iota(I32, (count, cols), 0), edge)
        lower = lane < cols // 2
        main = jnp.where(lower, here, beside)
        rims = pltpu.roll(jnp.where(lower, beside, here), cols // 2, 1)
        before = jnp.where(place == 0, rims, pltpu.roll(main, 1, 0))
        after = jnp.where(place == edge - 1, rims, pltpu.roll(main, count - 1, 0))
        window = jnp.concatenate([before, main, after], axis=1)
        high = window.astype(jnp.bfloat16)
        low = (window - high.astype(F32)).astype(jnp.bfloat16)
        weight = gates[...]
        preact = jnp.dot(high, weight, preferred_element_type=F32) + jnp.dot(
            low, weight, preferred_element_type=F32
        )
        retain = jax.nn.sigmoid(preact[:, :span] + bias_z)
        fresh = (1.0 - retain) * jnp.tanh(preact[:, span:] + bias_c)

        def planes(x):
            pair = [x[:, :cols], x[:, cols:]]
            return [pair[0], pltpu.roll(pair[0], cols // 2, 1), pair[1], pltpu.roll(pair[1], cols // 2, 1)]

        keep, new = planes(retain), planes(fresh)
        decay, offset = [keep[0]], [new[0]]
        for p in range(1, PD):
            decay.append(keep[p] * decay[-1])
            offset.append(keep[p] * offset[-1] + new[p])
        if once:
            state, entries = jnp.zeros((edge, cols), F32), []
            for i in range(n):
                entries.append(state)
                at = slice(i * edge, (i + 1) * edge)
                state = decay[-1][at] * state + offset[-1][at]
            start = jnp.concatenate(entries, axis=0)
        else:
            own_recv[...] = decay[-1].reshape(n, edge, cols)
            side_recv[...] = offset[-1].reshape(n, edge, cols)

            def compose(i, state):
                entry[i] = state
                return own_recv[i] * state + side_recv[i]

            lax.fori_loop(0, n, compose, jnp.zeros((edge, cols), F32))
            start = entry[...].reshape(count, cols)
        states = [decay[p] * start + offset[p] for p in range(PD)]
        states = jnp.concatenate(
            [
                jnp.where(lower, states[p], pltpu.roll(states[p + 1], cols // 2, 1))
                for p in range(0, PD, 2)
            ],
            axis=1,
        )
        high = states.astype(jnp.bfloat16)
        low = (states - high.astype(F32)).astype(jnp.bfloat16)
        scores = jnp.dot(low, out_high, preferred_element_type=F32) + jnp.dot(
            high, out_low, preferred_element_type=F32
        )
        scores = scores + jnp.dot(high, out_high, preferred_element_type=F32)
        scores = scores.reshape(n, edge, cols)

        def over_planes(x, combine):
            x = combine(x, pltpu.roll(x, rows, 1))
            return combine(x, pltpu.roll(x, 2 * rows, 1))

        highest = over_planes(jnp.max(scores, axis=0), jnp.maximum)
        weights = jnp.exp(scores - highest[None])
        total = over_planes(jnp.sum(weights, axis=0), jnp.add)
        shape = (n, edge, cols)
        plane = lax.rem(lax.broadcasted_iota(I32, shape, 2), PD * rows) // rows
        plane = (plane + PD * lax.broadcasted_iota(I32, shape, 0)).astype(F32)
        value = 1.0 / (0.1 + 0.9 * plane / (PD * n - 1))
        depth = over_planes(jnp.sum(weights * value, axis=0), jnp.add) / total
        first = lax.broadcasted_iota(I32, shape, 2) < PD * rows
        fin_send[...] = jnp.where(first, weights / total[None], depth[None])
        fin_recv[me] = fin_send[me]

        def send_fin(k, carry):
            to = far(k)
            push(fin_send.at[to], fin_recv.at[me], {"depth": to}, 4).start()
            return carry

        lax.fori_loop(0, n - 1, send_fin, 0, unroll=once)
        drain(fin_recv, holders - 1, 4, recv_sems)

    hold() if n == holders else pl.when(me < holders)(hold)
    if n != holders:
        @pl.when(me >= holders)
        def _():
            drain(fin_recv, holders, 4, recv_sems)

    result = jnp.transpose(fin_recv[...].reshape(cols, cols))
    for r in range(rows):
        depth_ref[r : r + 1, :] = result[PD * rows + r : PD * rows + r + 1]
        for p in range(PD):
            prob_ref[p, r : r + 1, :] = result[p * rows + r : p * rows + r + 1]

    drain(tab_send, n - 1, 0, send_sems)
    drain(ans_send, cap * (n - 1), 1, send_sems)
    drain(side_send, holders, 3, send_sems)
    if n == holders:
        drain(own_send, n - 1, 2, send_sems)
        drain(fin_send, n - 1, 4, send_sems)
    else:
        @pl.when(me < holders)
        def _():
            drain(own_send, holders - 1, 2, send_sems)
            drain(fin_send, n - 1, 4, send_sems)

        @pl.when(me >= holders)
        def _():
            drain(own_send, holders, 2, send_sems)


def hand_over(prob_in, depth_in, prob_out, depth_out, sems):
    copies = [
        pltpu.make_async_copy(prob_in, prob_out, sems.at[0]),
        pltpu.make_async_copy(depth_in, depth_out, sems.at[1]),
    ]
    for copy in copies:
        copy.start()
    for copy in copies:
        copy.wait()


def body(ref_feat, src_feat, tile_owner, tile_local, col_shift, w_gates, bias_z, bias_c, w_out):
    n = lax.axis_size("depth")
    rows, feat, cols = ref_feat.shape
    groups = w_gates.shape[2]
    hidden = w_gates.shape[1] // 2
    requests = tile_owner.shape[0]
    cap = max(2, (3 * requests + 2 * n - 1) // (2 * n))
    tiles = (n, 8, cols)
    holders = (cols // 8, 8, cols)
    span = PD * rows * hidden
    anywhere = pl.BlockSpec(memory_space=pl.ANY)
    vmem = pl.BlockSpec(memory_space=pltpu.VMEM)
    shapes = (
        jax.ShapeDtypeStruct((PD, rows, cols), F32),
        jax.ShapeDtypeStruct((rows, cols), F32),
    )
    results = pl.pallas_call(
        functools.partial(kernel, n, cap),
        out_shape=shapes,
        in_specs=[anywhere] * 9,
        out_specs=(vmem, vmem),
        scratch_shapes=[
            pltpu.VMEM(ref_feat.shape, ref_feat.dtype),
            pltpu.VMEM(src_feat.shape, src_feat.dtype),
            pltpu.VMEM((1, requests), I32),
            pltpu.VMEM((1, requests), I32),
            pltpu.VMEM((1, requests), I32),
            pltpu.VMEM((9, groups, 2 * hidden), w_gates.dtype),
            pltpu.VMEM((1, hidden), F32),
            pltpu.VMEM((1, hidden), F32),
            pltpu.VMEM((1, hidden), F32),
            pltpu.VMEM(src_feat.shape, F32),
            pltpu.VMEM(ref_feat.shape, F32),
            pltpu.VMEM((n, 1, cols), I32),
            pltpu.VMEM((n, 1, cols), I32),
            pltpu.SMEM((n, 1, cols), I32),
            pltpu.VMEM((1, cols), I32),
            pltpu.SMEM((1, cols), I32),
            pltpu.VMEM((8, feat, cols), F32),
            pltpu.VMEM((n * cap, groups, cols), F32),
            pltpu.VMEM((n * cap, groups, cols), F32),
            pltpu.VMEM((3 * cols, 2 * span), F32),
            pltpu.VMEM((3 * cols, 2 * span), jnp.bfloat16),
            pltpu.VMEM(holders, F32),
            pltpu.VMEM(tiles, F32),
            pltpu.VMEM(holders, F32),
            pltpu.VMEM(tiles, F32),
            pltpu.VMEM(tiles, F32),
            pltpu.VMEM(tiles, F32),
            pltpu.VMEM(holders, F32),
            pltpu.SemaphoreType.DMA((9,)),
            pltpu.SemaphoreType.DMA((2,)),
            pltpu.SemaphoreType.DMA((5,)),
            pltpu.SemaphoreType.DMA((5,)),
        ],
        compiler_params=pltpu.CompilerParams(
            collective_id=0, has_side_effects=True, vmem_limit_bytes=60 * 1024 * 1024
        ),
        cost_estimate=pl.CostEstimate(
            flops=2 * 144 * 64 * 1024, bytes_accessed=src_feat.size * 2, transcendentals=65536
        ),
    )(
        ref_feat, src_feat, tile_owner.reshape(1, requests), tile_local.reshape(1, requests),
        col_shift.reshape(1, requests), jnp.transpose(w_gates, (0, 2, 1)), bias_z.reshape(1, hidden),
        bias_c.reshape(1, hidden), w_out.reshape(1, hidden),
    )
    return pl.pallas_call(
        hand_over,
        out_shape=shapes,
        in_specs=[anywhere] * 2,
        out_specs=(anywhere, anywhere),
        scratch_shapes=[pltpu.SemaphoreType.DMA((2,))],
        compiler_params=pltpu.CompilerParams(vmem_limit_bytes=60 * 1024 * 1024),
    )(*results)


def solution(mesh):
    return jax.shard_map(
        body,
        mesh=mesh,
        in_specs=(
            P("slab", None, None),
            P("depth", None, None),
            P(("depth", "slab"), None),
            P(("depth", "slab")),
            P(("depth", "slab")),
            P(),
            P(),
            P(),
            P(),
        ),
        out_specs=(P("depth", "slab", None), P("slab", None)),
        check_vma=False,
    )
```

```python
import functools

import jax
import jax.numpy as jnp
from jax import lax
from jax.experimental import pallas as pl
from jax.experimental.pallas import tpu as pltpu
from jax.sharding import PartitionSpec as P

VIEWS = 5
PD = 4
MAXSHIFT = 16
MESH = pl.DeviceIdType.MESH
F32 = jnp.float32
I32 = jnp.int32


def kernel(
    n, cap,
    ref_hbm, src_hbm, owner_hbm, local_hbm, shift_hbm, w_hbm, bz_hbm, bc_hbm, wo_hbm,
    fin_recv,
    ref_ref, src, owner_ref, local_ref, shift_ref, w_ref, bz_ref, bc_ref, wo_ref,
    ref_wide, tab_send, tab_recv, tab_s, own_v, own_s, prod, ans_send, ans_recv,
    gates_wide, gates, own_send, own_recv, side_send, side_recv, entry, fin_send,
    in_sems, smem_sems, send_sems, recv_sems,
):
    me = lax.axis_index("depth")
    slab = lax.axis_index("slab")
    requests = owner_ref.shape[1]
    rows, feat, cols = ref_ref.shape
    groups = w_ref.shape[1]
    hidden = w_ref.shape[2] // 2
    cpg = feat // groups

    edge = 8
    holders = cols // edge
    once = n <= 16

    def peer(k):
        return lax.rem(me + k, n)

    def far(j):
        step = (j + 1) // 2
        return peer(n // 2 + jnp.where(lax.rem(j, 2) == 1, -step, step))

    pairs = [
        (owner_hbm, owner_ref), (local_hbm, local_ref), (shift_hbm, shift_ref), (ref_hbm, ref_ref),
        (src_hbm, src), (w_hbm, w_ref), (bz_hbm, bz_ref), (bc_hbm, bc_ref), (wo_hbm, wo_ref),
    ]
    loads = [pltpu.make_async_copy(a, b, in_sems.at[i]) for i, (a, b) in enumerate(pairs)]
    for load in loads:
        load.start()
    barrier = pltpu.get_barrier_semaphore()

    def greet(k, carry):
        pl.semaphore_signal(barrier, inc=1, device_id={"depth": peer(k)}, device_id_type=MESH)
        return carry

    def greet_side(k, carry):
        who = {"depth": peer(k), "slab": 1 - slab}
        pl.semaphore_signal(barrier, inc=1, device_id=who, device_id_type=MESH)
        return carry

    lax.fori_loop(1, n, greet, 0, unroll=once)
    lax.fori_loop(0, n, greet_side, 0, unroll=once)

    q_sub = lax.broadcasted_iota(I32, (requests, requests), 0)
    q_lane = lax.broadcasted_iota(I32, (requests, requests), 1)
    diag = q_sub == q_lane
    for load in loads[:3]:
        load.wait()
    owner_row = owner_ref[...]
    owner_col = jnp.sum(
        jnp.where(diag, owner_row, 0).astype(F32), axis=1, keepdims=True
    ).astype(I32)
    local_col = jnp.sum(jnp.where(diag, local_ref[...], 0).astype(F32), axis=1, keepdims=True)
    shift_col = jnp.sum(
        jnp.where(diag, shift_ref[...] + MAXSHIFT, 0).astype(F32), axis=1, keepdims=True
    )
    same = (owner_row == owner_col) & (q_lane < q_sub)
    slot_col = jnp.sum(jnp.where(same, 1.0, 0.0), axis=1, keepdims=True)
    lane = lax.broadcasted_iota(I32, (requests, cols), 1)
    row_col = lax.rem(lax.broadcasted_iota(I32, (requests, cols), 0), rows).astype(F32)
    kind = lane // cap
    value = jnp.where(
        kind == 0, local_col, jnp.where(kind == 1, shift_col, jnp.where(kind == 2, row_col, 0.0))
    )
    value = jnp.where(lax.rem(lane, cap).astype(F32) == slot_col, value, 0.0)
    owner_hot = jnp.where(
        lax.broadcasted_iota(I32, (n, requests), 0) == owner_row, 1.0, 0.0
    )
    table = jnp.dot(
        owner_hot.astype(jnp.bfloat16), value.astype(jnp.bfloat16), preferred_element_type=F32
    ).astype(I32)
    tab_send[:, 0, :] = table
    place_col = owner_col.astype(F32) * cap + slot_col
    wide_diag = lax.broadcasted_iota(I32, (requests, cols), 0) == lane
    own_v[...] = jnp.sum(jnp.where(wide_diag, place_col, 0.0), axis=0, keepdims=True).astype(I32)
    own_copy = pltpu.make_async_copy(own_v, own_s, smem_sems.at[0])
    own_copy.start()

    def push(source, target, who, number):
        return pltpu.make_async_remote_copy(
            src_ref=source, dst_ref=target, send_sem=send_sems.at[number],
            recv_sem=recv_sems.at[number], device_id=who, device_id_type=MESH,
        )

    def drain(buffer, count, number, sems):
        part = buffer.at[pl.ds(0, count)]
        pltpu.make_async_copy(part, part, sems.at[number]).wait()

    pl.semaphore_wait(barrier, 2 * n - 1)

    def send_table(k, carry):
        to = far(k)
        push(tab_send.at[to], tab_recv.at[me], {"depth": to}, 0).start()
        return carry

    lax.fori_loop(0, n - 1, send_table, 0, unroll=once)
    tab_recv[me] = tab_send[me]
    for load in loads[3:5]:
        load.wait()

    def regroup(at):
        return [prod[at, pl.ds(c, groups, stride=cpg), :] for c in range(cpg)]

    for r in range(rows):
        prod[r] = ref_ref[r].astype(F32)
    for r in range(rows):
        ref_wide[r] = jnp.concatenate(regroup(r), axis=0)
    drain(tab_recv, n - 1, 0, recv_sems)
    tab_copy = pltpu.make_async_copy(tab_recv, tab_s, smem_sems.at[1])
    tab_copy.start()
    tab_copy.wait()

    position = lax.broadcasted_iota(I32, (groups, cols), 1)

    def correlate(who, out, at):
        tiles, shifts, picked = [], [], []
        for s in range(cap):
            tiles.append(jnp.clip(tab_s[who, 0, s], 0, src.shape[0] - 1))
            shifts.append(jnp.clip(tab_s[who, 0, cap + s], 0, 2 * MAXSHIFT) - MAXSHIFT)
            picked.append(jnp.clip(tab_s[who, 0, 2 * cap + s], 0, rows - 1))
        for s in range(cap):
            prod[s] = src[tiles[s]].astype(F32)
        wide = [jnp.concatenate(regroup(s), axis=0) for s in range(cap)]
        moved = [pltpu.roll(wide[s], lax.rem(shifts[s] + cols, cols), 1) for s in range(cap)]
        for s in range(cap):
            terms = moved[s] * ref_wide[picked[s]]
            total = terms[0:groups]
            for c in range(1, cpg):
                total = total + terms[c * groups : (c + 1) * groups]
            source_col = position - shifts[s]
            inside = (source_col >= 0) & (source_col < cols)
            out[at * cap + s] = jnp.where(inside, total, 0.0)

    def answer(k, carry):
        to = far(k)
        correlate(to, ans_send, to)
        push(
            ans_send.at[pl.ds(to * cap, cap)], ans_recv.at[pl.ds(me * cap, cap)], {"depth": to}, 1
        ).start()
        return carry

    lax.fori_loop(0, n - 1, answer, 0)
    correlate(me, ans_recv, me)
    for load in loads[5:]:
        load.wait()
    taps = [w_ref[t].astype(F32) for t in range(9)]
    span = PD * rows * hidden
    plane_of = lax.broadcasted_iota(I32, (groups, span), 1) // (rows * hidden)

    def fill(at, pieces):
        for kind in range(2):
            units = slice(kind * hidden, (kind + 1) * hidden)
            part = jnp.concatenate([x[:, units] for x in pieces] * PD, axis=1)
            for p in range(PD):
                gates_wide[pl.ds(at(p), groups), pl.ds(kind * span, span)] = jnp.where(
                    plane_of == p, part, 0.0
                )

    own_rows = PD * rows * groups
    for b in range(3):
        for r in range(rows):
            fill(
                lambda p: b * cols + (p * rows + r) * groups,
                [taps[(r - to + 1) * 3 + b] for to in range(rows)],
            )
        pieces = [jnp.zeros((groups, 2 * hidden), F32) for _ in range(rows)]
        pieces[0] = pieces[0] + jnp.where(slab == 1, taps[b], 0.0)
        pieces[-1] = pieces[-1] + jnp.where(slab == 0, taps[6 + b], 0.0)
        fill(lambda p: b * cols + own_rows + p * groups, pieces)
        rest = own_rows + PD * groups
        gates_wide[pl.ds(b * cols + rest, cols - rest), :] = jnp.zeros((cols - rest, 2 * span), F32)
    gates[...] = gates_wide[...].astype(jnp.bfloat16)
    bias_z = jnp.concatenate([bz_ref[...]] * (PD * rows), axis=1)
    bias_c = jnp.concatenate([bc_ref[...]] * (PD * rows), axis=1)
    h_eye = lax.broadcasted_iota(I32, (hidden, hidden), 0) == lax.broadcasted_iota(
        I32, (hidden, hidden), 1
    )
    out_col = jnp.sum(jnp.where(h_eye, wo_ref[...], 0.0), axis=1, keepdims=True)
    out_col = jnp.concatenate([out_col] * (PD * rows), axis=0)
    unit_block = lax.broadcasted_iota(I32, (span, cols), 0) // hidden
    lane_block = lax.rem(lax.broadcasted_iota(I32, (span, cols), 1), PD * rows)
    out_wide = jnp.where(unit_block == lane_block, out_col, 0.0)
    out_high = out_wide.astype(jnp.bfloat16)
    out_low = (out_wide - out_high.astype(F32)).astype(jnp.bfloat16)
    own_copy.wait()
    drain(ans_recv, cap * (n - 1), 1, recv_sems)

    scale = 1.0 / (VIEWS * cpg)
    cost = {}
    for p in range(PD):
        for r in range(rows):
            total = None
            for v in range(VIEWS):
                place = jnp.clip(own_s[0, (p * VIEWS + v) * rows + r], 0, n * cap - 1)
                term = ans_recv[place]
                total = term if total is None else total + term
            cost[p, r] = total * scale

    in_block = lax.rem(position, edge)

    def rim(x):
        left = jnp.where(position == 0, 0.0, pltpu.roll(x, 1, 1))
        right = jnp.where(position == cols - 1, 0.0, pltpu.roll(x, cols - 1, 1))
        return jnp.where(in_block == 0, left, right)

    blocks = [cost[p, r] for p in range(PD) for r in range(rows)]
    near = [jnp.where(slab == 0, cost[p, rows - 1], cost[p, 0]) for p in range(PD)]
    gap = jnp.zeros((cols // 2 - PD * groups, cols), F32)
    side = jnp.concatenate([rim(x) for x in near] + [gap] + near + [gap], axis=0)
    side_send[...] = jnp.transpose(side).reshape(holders, edge, cols)

    def send_side(k, carry):
        to = far(k) if n == holders else k
        who = {"depth": to, "slab": 1 - slab}
        push(side_send.at[to], side_recv.at[me], who, 3).start()
        return carry

    own = jnp.concatenate(blocks + [rim(x) for x in blocks], axis=0)
    own_send[...] = jnp.transpose(own).reshape(holders, edge, cols)

    def send_own(k, carry):
        to = far(k) if n == holders else k

        def go():
            push(own_send.at[to], own_recv.at[me], {"depth": to}, 2).start()

        go() if n == holders else pl.when(to != me)(go)
        return carry

    if n == holders:
        def send_both(k, carry):
            send_own(k, carry)
            return send_side(k, carry)

        lax.fori_loop(0, n - 1, send_both, 0, unroll=once)
        push(side_send.at[me], side_recv.at[me], {"depth": me, "slab": 1 - slab}, 3).start()
    else:
        lax.fori_loop(0, holders, send_own, 0)
        lax.fori_loop(0, holders, send_side, 0)

    def hold():
        own_recv[me] = own_send[me]
        drain(own_recv, n - 1, 2, recv_sems)
        drain(side_recv, n, 3, recv_sems)
        count = n * edge
        here = own_recv[...].reshape(count, cols)
        beside = side_recv[...].reshape(count, cols)
        lane = lax.broadcasted_iota(I32, (count, cols), 1)
        place = lax.rem(lax.broadcasted_iota(I32, (count, cols), 0), edge)
        lower = lane < cols // 2
        main = jnp.where(lower, here, beside)
        rims = pltpu.roll(jnp.where(lower, beside, here), cols // 2, 1)
        before = jnp.where(place == 0, rims, pltpu.roll(main, 1, 0))
        after = jnp.where(place == edge - 1, rims, pltpu.roll(main, count - 1, 0))
        window = jnp.concatenate([before, main, after], axis=1)
        high = window.astype(jnp.bfloat16)
        low = (window - high.astype(F32)).astype(jnp.bfloat16)
        both = jnp.dot(
            jnp.concatenate([high, low], axis=0), gates[...], preferred_element_type=F32
        )
        preact = both[:count] + both[count:]
        retain = jax.nn.sigmoid(preact[:, :span] + bias_z)
        fresh = (1.0 - retain) * jnp.tanh(preact[:, span:] + bias_c)

        def planes(x):
            pair = [x[:, :cols], x[:, cols:]]
            return [pair[0], pltpu.roll(pair[0], cols // 2, 1), pair[1], pltpu.roll(pair[1], cols // 2, 1)]

        keep, new = planes(retain), planes(fresh)
        decay, offset = [keep[0]], [new[0]]
        for p in range(1, PD):
            decay.append(keep[p] * decay[-1])
            offset.append(keep[p] * offset[-1] + new[p])
        if once:
            state, entries = jnp.zeros((edge, cols), F32), []
            for i in range(n):
                entries.append(state)
                at = slice(i * edge, (i + 1) * edge)
                state = decay[-1][at] * state + offset[-1][at]
            start = jnp.concatenate(entries, axis=0)
        else:
            own_recv[...] = decay[-1].reshape(n, edge, cols)
            side_recv[...] = offset[-1].reshape(n, edge, cols)

            def compose(i, state):
                entry[i] = state
                return own_recv[i] * state + side_recv[i]

            lax.fori_loop(0, n, compose, jnp.zeros((edge, cols), F32))
            start = entry[...].reshape(count, cols)
        states = [decay[p] * start + offset[p] for p in range(PD)]
        states = jnp.concatenate(
            [
                jnp.where(lower, states[p], pltpu.roll(states[p + 1], cols // 2, 1))
                for p in range(0, PD, 2)
            ],
            axis=1,
        )
        high = states.astype(jnp.bfloat16)
        low = (states - high.astype(F32)).astype(jnp.bfloat16)
        scores = jnp.dot(low, out_high, preferred_element_type=F32) + jnp.dot(
            high, out_low, preferred_element_type=F32
        )
        scores = scores + jnp.dot(high, out_high, preferred_element_type=F32)
        scores = scores.reshape(n, edge, cols)

        def over_planes(x, combine):
            x = combine(x, pltpu.roll(x, rows, 1))
            return combine(x, pltpu.roll(x, 2 * rows, 1))

        highest = over_planes(jnp.max(scores, axis=0), jnp.maximum)
        weights = jnp.exp(scores - highest[None])
        total = over_planes(jnp.sum(weights, axis=0), jnp.add)
        shape = (n, edge, cols)
        plane = lax.rem(lax.broadcasted_iota(I32, shape, 2), PD * rows) // rows
        plane = (plane + PD * lax.broadcasted_iota(I32, shape, 0)).astype(F32)
        value = 1.0 / (0.1 + 0.9 * plane / (PD * n - 1))
        depth = over_planes(jnp.sum(weights * value, axis=0), jnp.add) / total
        first = lax.broadcasted_iota(I32, shape, 2) < PD * rows
        fin_send[...] = jnp.where(first, weights / total[None], depth[None])
        fin_own = pltpu.make_async_copy(fin_send.at[me], fin_recv.at[me], smem_sems.at[1])
        fin_own.start()

        def send_fin(k, carry):
            to = far(k)
            push(fin_send.at[to], fin_recv.at[me], {"depth": to}, 4).start()
            return carry

        lax.fori_loop(0, n - 1, send_fin, 0, unroll=once)
        fin_own.wait()
        drain(fin_recv, holders - 1, 4, recv_sems)

    hold() if n == holders else pl.when(me < holders)(hold)
    if n != holders:
        @pl.when(me >= holders)
        def _():
            drain(fin_recv, holders, 4, recv_sems)

    drain(tab_send, n - 1, 0, send_sems)
    drain(ans_send, cap * (n - 1), 1, send_sems)
    drain(side_send, holders, 3, send_sems)
    if n == holders:
        drain(own_send, n - 1, 2, send_sems)
        drain(fin_send, n - 1, 4, send_sems)
    else:
        @pl.when(me < holders)
        def _():
            drain(own_send, holders - 1, 2, send_sems)
            drain(fin_send, n - 1, 4, send_sems)

        @pl.when(me >= holders)
        def _():
            drain(own_send, holders, 2, send_sems)


def hand_over(fin_ref, prob_ref, depth_ref):
    planes, rows, cols = prob_ref.shape
    result = jnp.transpose(fin_ref[...].reshape(cols, cols))
    for r in range(rows):
        depth_ref[r : r + 1, :] = result[planes * rows + r : planes * rows + r + 1]
        for p in range(planes):
            prob_ref[p, r : r + 1, :] = result[p * rows + r : p * rows + r + 1]


def body(ref_feat, src_feat, tile_owner, tile_local, col_shift, w_gates, bias_z, bias_c, w_out):
    n = lax.axis_size("depth")
    rows, feat, cols = ref_feat.shape
    groups = w_gates.shape[2]
    hidden = w_gates.shape[1] // 2
    requests = tile_owner.shape[0]
    cap = max(2, (3 * requests + 2 * n - 1) // (2 * n))
    tiles = (n, 8, cols)
    holders = (cols // 8, 8, cols)
    span = PD * rows * hidden
    anywhere = pl.BlockSpec(memory_space=pl.ANY)
    vmem = pl.BlockSpec(memory_space=pltpu.VMEM)
    shapes = (
        jax.ShapeDtypeStruct((PD, rows, cols), F32),
        jax.ShapeDtypeStruct((rows, cols), F32),
    )
    landed = pl.pallas_call(
        functools.partial(kernel, n, cap),
        out_shape=jax.ShapeDtypeStruct(holders, F32),
        in_specs=[anywhere] * 9,
        out_specs=anywhere,
        scratch_shapes=[
            pltpu.VMEM(ref_feat.shape, ref_feat.dtype),
            pltpu.VMEM(src_feat.shape, src_feat.dtype),
            pltpu.VMEM((1, requests), I32),
            pltpu.VMEM((1, requests), I32),
            pltpu.VMEM((1, requests), I32),
            pltpu.VMEM((9, groups, 2 * hidden), w_gates.dtype),
            pltpu.VMEM((1, hidden), F32),
            pltpu.VMEM((1, hidden), F32),
            pltpu.VMEM((1, hidden), F32),
            pltpu.VMEM(ref_feat.shape, F32),
            pltpu.VMEM((n, 1, cols), I32),
            pltpu.VMEM((n, 1, cols), I32),
            pltpu.SMEM((n, 1, cols), I32),
            pltpu.VMEM((1, cols), I32),
            pltpu.SMEM((1, cols), I32),
            pltpu.VMEM((cap, feat, cols), F32),
            pltpu.VMEM((n * cap, groups, cols), F32),
            pltpu.VMEM((n * cap, groups, cols), F32),
            pltpu.VMEM((3 * cols, 2 * span), F32),
            pltpu.VMEM((3 * cols, 2 * span), jnp.bfloat16),
            pltpu.VMEM(holders, F32),
            pltpu.VMEM(tiles, F32),
            pltpu.VMEM(holders, F32),
            pltpu.VMEM(tiles, F32),
            pltpu.VMEM(tiles, F32),
            pltpu.VMEM(tiles, F32),
            pltpu.SemaphoreType.DMA((9,)),
            pltpu.SemaphoreType.DMA((2,)),
            pltpu.SemaphoreType.DMA((5,)),
            pltpu.SemaphoreType.DMA((5,)),
        ],
        compiler_params=pltpu.CompilerParams(
            collective_id=0, has_side_effects=True, vmem_limit_bytes=60 * 1024 * 1024
        ),
        cost_estimate=pl.CostEstimate(
            flops=2 * 144 * 64 * 1024, bytes_accessed=src_feat.size * 2, transcendentals=65536
        ),
    )(
        ref_feat, src_feat, tile_owner.reshape(1, requests), tile_local.reshape(1, requests),
        col_shift.reshape(1, requests), jnp.transpose(w_gates, (0, 2, 1)), bias_z.reshape(1, hidden),
        bias_c.reshape(1, hidden), w_out.reshape(1, hidden),
    )
    return pl.pallas_call(
        hand_over,
        out_shape=shapes,
        in_specs=[vmem],
        out_specs=(vmem, vmem),
        compiler_params=pltpu.CompilerParams(vmem_limit_bytes=60 * 1024 * 1024),
    )(landed)


def solution(mesh):
    return jax.shard_map(
        body,
        mesh=mesh,
        in_specs=(
            P("slab", None, None),
            P("depth", None, None),
            P(("depth", "slab"), None),
            P(("depth", "slab")),
            P(("depth", "slab")),
            P(),
            P(),
            P(),
            P(),
        ),
        out_specs=(P("depth", "slab", None), P("slab", None)),
        check_vma=False,
    )
```

```python
import functools

import jax
import jax.numpy as jnp
from jax import lax
from jax.experimental import pallas as pl
from jax.experimental.pallas import tpu as pltpu
from jax.sharding import PartitionSpec as P

VIEWS = 5
PD = 4
MAXSHIFT = 16
MESH = pl.DeviceIdType.MESH
F32 = jnp.float32
I32 = jnp.int32


def kernel(
    n, cap,
    ref_hbm, src_hbm, owner_hbm, local_hbm, shift_hbm, w_hbm, bz_hbm, bc_hbm, wo_hbm,
    fin_recv,
    ref_ref, src, owner_ref, local_ref, shift_ref, w_ref, bz_ref, bc_ref, wo_ref,
    ref_wide, tab_send, tab_recv, tab_s, own_v, own_s, prod, code_send, code_recv,
    scale_send, scale_recv, answers,
    gates_wide, gates, own_send, own_recv, side_send, side_recv, entry, fin_send,
    in_sems, smem_sems, send_sems, recv_sems,
):
    me = lax.axis_index("depth")
    slab = lax.axis_index("slab")
    requests = owner_ref.shape[1]
    rows, feat, cols = ref_ref.shape
    groups = w_ref.shape[1]
    hidden = w_ref.shape[2] // 2
    cpg = feat // groups

    edge = 8
    holders = cols // edge
    once = n <= 16

    def peer(k):
        return lax.rem(me + k, n)

    def far(j):
        step = (j + 1) // 2
        return peer(n // 2 + jnp.where(lax.rem(j, 2) == 1, -step, step))

    pairs = [
        (owner_hbm, owner_ref), (local_hbm, local_ref), (shift_hbm, shift_ref), (ref_hbm, ref_ref),
        (src_hbm, src), (w_hbm, w_ref), (bz_hbm, bz_ref), (bc_hbm, bc_ref), (wo_hbm, wo_ref),
    ]
    loads = [pltpu.make_async_copy(a, b, in_sems.at[i]) for i, (a, b) in enumerate(pairs)]
    for load in loads:
        load.start()
    barrier = pltpu.get_barrier_semaphore()

    def greet(k, carry):
        pl.semaphore_signal(barrier, inc=1, device_id={"depth": peer(k)}, device_id_type=MESH)
        return carry

    def greet_side(k, carry):
        who = {"depth": peer(k), "slab": 1 - slab}
        pl.semaphore_signal(barrier, inc=1, device_id=who, device_id_type=MESH)
        return carry

    lax.fori_loop(1, n, greet, 0, unroll=once)
    lax.fori_loop(0, n, greet_side, 0, unroll=once)

    q_sub = lax.broadcasted_iota(I32, (requests, requests), 0)
    q_lane = lax.broadcasted_iota(I32, (requests, requests), 1)
    diag = q_sub == q_lane
    for load in loads[:3]:
        load.wait()
    owner_row = owner_ref[...]
    owner_col = jnp.sum(
        jnp.where(diag, owner_row, 0).astype(F32), axis=1, keepdims=True
    ).astype(I32)
    local_col = jnp.sum(jnp.where(diag, local_ref[...], 0).astype(F32), axis=1, keepdims=True)
    shift_col = jnp.sum(
        jnp.where(diag, shift_ref[...] + MAXSHIFT, 0).astype(F32), axis=1, keepdims=True
    )
    same = (owner_row == owner_col) & (q_lane < q_sub)
    slot_col = jnp.sum(jnp.where(same, 1.0, 0.0), axis=1, keepdims=True)
    lane = lax.broadcasted_iota(I32, (requests, cols), 1)
    row_col = lax.rem(lax.broadcasted_iota(I32, (requests, cols), 0), rows).astype(F32)
    kind = lane // cap
    value = jnp.where(
        kind == 0, local_col, jnp.where(kind == 1, shift_col, jnp.where(kind == 2, row_col, 0.0))
    )
    value = jnp.where(lax.rem(lane, cap).astype(F32) == slot_col, value, 0.0)
    owner_hot = jnp.where(
        lax.broadcasted_iota(I32, (n, requests), 0) == owner_row, 1.0, 0.0
    )
    table = jnp.dot(
        owner_hot.astype(jnp.bfloat16), value.astype(jnp.bfloat16), preferred_element_type=F32
    ).astype(I32)
    tab_send[:, 0, :] = table
    place_col = owner_col.astype(F32) * cap + slot_col
    wide_diag = lax.broadcasted_iota(I32, (requests, cols), 0) == lane
    own_v[...] = jnp.sum(jnp.where(wide_diag, place_col, 0.0), axis=0, keepdims=True).astype(I32)
    own_copy = pltpu.make_async_copy(own_v, own_s, smem_sems.at[0])
    own_copy.start()

    def push(source, target, who, number):
        return pltpu.make_async_remote_copy(
            src_ref=source, dst_ref=target, send_sem=send_sems.at[number],
            recv_sem=recv_sems.at[number], device_id=who, device_id_type=MESH,
        )

    def drain(buffer, count, number, sems):
        part = buffer.at[pl.ds(0, count)]
        pltpu.make_async_copy(part, part, sems.at[number]).wait()

    pl.semaphore_wait(barrier, 2 * n - 1)

    def send_table(k, carry):
        to = far(k)
        push(tab_send.at[to], tab_recv.at[me], {"depth": to}, 0).start()
        return carry

    lax.fori_loop(0, n - 1, send_table, 0, unroll=once)
    tab_recv[me] = tab_send[me]
    for load in loads[3:5]:
        load.wait()

    def regroup(at):
        return [prod[at, pl.ds(c, groups, stride=cpg), :] for c in range(cpg)]

    for r in range(rows):
        prod[r] = ref_ref[r].astype(F32)
    for r in range(rows):
        ref_wide[r] = jnp.concatenate(regroup(r), axis=0)
    drain(tab_recv, n - 1, 0, recv_sems)
    tab_copy = pltpu.make_async_copy(tab_recv, tab_s, smem_sems.at[1])
    tab_copy.start()
    tab_copy.wait()

    position = lax.broadcasted_iota(I32, (groups, cols), 1)

    top_code = 32767.0

    def correlate(whos):
        slots = [(who, s) for who in whos for s in range(cap)]
        tiles, shifts, picked = [], [], []
        for who, s in slots:
            tiles.append(jnp.clip(tab_s[who, 0, s], 0, src.shape[0] - 1))
            shifts.append(jnp.clip(tab_s[who, 0, cap + s], 0, 2 * MAXSHIFT) - MAXSHIFT)
            picked.append(jnp.clip(tab_s[who, 0, 2 * cap + s], 0, rows - 1))
        for i, tile in enumerate(tiles):
            prod[i] = src[tile].astype(F32)
        wide = [jnp.concatenate(regroup(i), axis=0) for i in range(len(slots))]
        moved = [pltpu.roll(x, lax.rem(y + cols, cols), 1) for x, y in zip(wide, shifts)]
        totals = []
        for i in range(len(slots)):
            terms = moved[i] * ref_wide[picked[i]]
            total = terms[0:groups]
            for c in range(1, cpg):
                total = total + terms[c * groups : (c + 1) * groups]
            source_col = position - shifts[i]
            inside = (source_col >= 0) & (source_col < cols)
            totals.append(jnp.where(inside, total, 0.0))
        return [totals[i * cap : (i + 1) * cap] for i in range(len(whos))]

    code_rows = cap * groups

    def dispatch(to, totals):
        codes = []
        for s, total in enumerate(totals):
            largest = jnp.maximum(jnp.max(jnp.abs(total), axis=0, keepdims=True), 1e-30)
            codes.append(jnp.round(total * (top_code / largest)).astype(I32))
            scale_send[to, s : s + 1, :] = largest * (1.0 / (top_code * VIEWS * cpg))
        at = pl.ds(pl.multiple_of(to * code_rows, code_rows), code_rows)
        code_send[at, :] = jnp.concatenate(codes, axis=0).astype(jnp.int16)
        home = pl.ds(pl.multiple_of(me * code_rows, code_rows), code_rows)
        push(code_send.at[at], code_recv.at[home], {"depth": to}, 1).start()
        push(scale_send.at[to], scale_recv.at[me], {"depth": to}, 5).start()

    def answer(k, carry):
        pair = [far(2 * k), far(2 * k + 1)]
        for to, totals in zip(pair, correlate(pair)):
            dispatch(to, totals)
        return carry

    lax.fori_loop(0, (n - 1) // 2, answer, 0)
    last = far(n - 2)
    for_last, for_me = correlate([last, me])
    dispatch(last, for_last)
    for s in range(cap):
        answers[me * cap + s] = for_me[s] * (1.0 / (VIEWS * cpg))
    for load in loads[5:]:
        load.wait()
    taps = [w_ref[t].astype(F32) for t in range(9)]
    span = PD * rows * hidden
    plane_of = lax.broadcasted_iota(I32, (groups, span), 1) // (rows * hidden)

    def fill(at, pieces):
        for kind in range(2):
            units = slice(kind * hidden, (kind + 1) * hidden)
            part = jnp.concatenate([x[:, units] for x in pieces] * PD, axis=1)
            for p in range(PD):
                gates_wide[pl.ds(at(p), groups), pl.ds(kind * span, span)] = jnp.where(
                    plane_of == p, part, 0.0
                )

    own_rows = PD * rows * groups
    for b in range(3):
        for r in range(rows):
            fill(
                lambda p: b * cols + (p * rows + r) * groups,
                [taps[(r - to + 1) * 3 + b] for to in range(rows)],
            )
        pieces = [jnp.zeros((groups, 2 * hidden), F32) for _ in range(rows)]
        pieces[0] = pieces[0] + jnp.where(slab == 1, taps[b], 0.0)
        pieces[-1] = pieces[-1] + jnp.where(slab == 0, taps[6 + b], 0.0)
        fill(lambda p: b * cols + own_rows + p * groups, pieces)
        rest = own_rows + PD * groups
        gates_wide[pl.ds(b * cols + rest, cols - rest), :] = jnp.zeros((cols - rest, 2 * span), F32)
    gates[...] = gates_wide[...].astype(jnp.bfloat16)
    bias_z = jnp.concatenate([bz_ref[...]] * (PD * rows), axis=1)
    bias_c = jnp.concatenate([bc_ref[...]] * (PD * rows), axis=1)
    h_eye = lax.broadcasted_iota(I32, (hidden, hidden), 0) == lax.broadcasted_iota(
        I32, (hidden, hidden), 1
    )
    out_col = jnp.sum(jnp.where(h_eye, wo_ref[...], 0.0), axis=1, keepdims=True)
    out_col = jnp.concatenate([out_col] * (PD * rows), axis=0)
    unit_block = lax.broadcasted_iota(I32, (span, cols), 0) // hidden
    lane_block = lax.rem(lax.broadcasted_iota(I32, (span, cols), 1), PD * rows)
    out_wide = jnp.where(unit_block == lane_block, out_col, 0.0)
    out_high = out_wide.astype(jnp.bfloat16)
    out_low = (out_wide - out_high.astype(F32)).astype(jnp.bfloat16)
    own_copy.wait()
    drain(code_recv, code_rows * (n - 1), 1, recv_sems)
    drain(scale_recv, n - 1, 5, recv_sems)

    def decode(k, carry):
        source = peer(k)
        at = pl.ds(pl.multiple_of(source * code_rows, code_rows), code_rows)
        values = code_recv[at, :].astype(I32).astype(F32)
        for s in range(cap):
            part = values[s * groups : (s + 1) * groups]
            answers[source * cap + s] = part * scale_recv[source, s : s + 1, :]
        return carry

    lax.fori_loop(1, n, decode, 0, unroll=once)
    cost = {}
    for p in range(PD):
        for r in range(rows):
            total = None
            for v in range(VIEWS):
                place = jnp.clip(own_s[0, (p * VIEWS + v) * rows + r], 0, n * cap - 1)
                term = answers[place]
                total = term if total is None else total + term
            cost[p, r] = total

    in_block = lax.rem(position, edge)

    def rim(x):
        left = jnp.where(position == 0, 0.0, pltpu.roll(x, 1, 1))
        right = jnp.where(position == cols - 1, 0.0, pltpu.roll(x, cols - 1, 1))
        return jnp.where(in_block == 0, left, right)

    blocks = [cost[p, r] for p in range(PD) for r in range(rows)]
    near = [jnp.where(slab == 0, cost[p, rows - 1], cost[p, 0]) for p in range(PD)]
    gap = jnp.zeros((cols // 2 - PD * groups, cols), F32)
    side = jnp.concatenate([rim(x) for x in near] + [gap] + near + [gap], axis=0)
    side_send[...] = jnp.transpose(side).reshape(holders, edge, cols)

    def send_side(k, carry):
        to = far(k) if n == holders else k
        who = {"depth": to, "slab": 1 - slab}
        push(side_send.at[to], side_recv.at[me], who, 3).start()
        return carry

    own = jnp.concatenate(blocks + [rim(x) for x in blocks], axis=0)
    own_send[...] = jnp.transpose(own).reshape(holders, edge, cols)

    def send_own(k, carry):
        to = far(k) if n == holders else k

        def go():
            push(own_send.at[to], own_recv.at[me], {"depth": to}, 2).start()

        go() if n == holders else pl.when(to != me)(go)
        return carry

    if n == holders:
        def send_both(k, carry):
            send_own(k, carry)
            return send_side(k, carry)

        lax.fori_loop(0, n - 1, send_both, 0, unroll=once)
        push(side_send.at[me], side_recv.at[me], {"depth": me, "slab": 1 - slab}, 3).start()
    else:
        lax.fori_loop(0, holders, send_own, 0)
        lax.fori_loop(0, holders, send_side, 0)

    def hold():
        own_recv[me] = own_send[me]
        drain(own_recv, n - 1, 2, recv_sems)
        drain(side_recv, n, 3, recv_sems)
        count = n * edge
        here = own_recv[...].reshape(count, cols)
        beside = side_recv[...].reshape(count, cols)
        lane = lax.broadcasted_iota(I32, (count, cols), 1)
        place = lax.rem(lax.broadcasted_iota(I32, (count, cols), 0), edge)
        lower = lane < cols // 2
        main = jnp.where(lower, here, beside)
        rims = pltpu.roll(jnp.where(lower, beside, here), cols // 2, 1)
        before = jnp.where(place == 0, rims, pltpu.roll(main, 1, 0))
        after = jnp.where(place == edge - 1, rims, pltpu.roll(main, count - 1, 0))
        window = jnp.concatenate([before, main, after], axis=1)
        high = window.astype(jnp.bfloat16)
        low = (window - high.astype(F32)).astype(jnp.bfloat16)
        both = jnp.dot(
            jnp.concatenate([high, low], axis=0), gates[...], preferred_element_type=F32
        )
        preact = both[:count] + both[count:]
        retain = jax.nn.sigmoid(preact[:, :span] + bias_z)
        fresh = (1.0 - retain) * jnp.tanh(preact[:, span:] + bias_c)

        def planes(x):
            pair = [x[:, :cols], x[:, cols:]]
            return [pair[0], pltpu.roll(pair[0], cols // 2, 1), pair[1], pltpu.roll(pair[1], cols // 2, 1)]

        keep, new = planes(retain), planes(fresh)
        decay, offset = [keep[0]], [new[0]]
        for p in range(1, PD):
            decay.append(keep[p] * decay[-1])
            offset.append(keep[p] * offset[-1] + new[p])
        if once:
            state, entries = jnp.zeros((edge, cols), F32), []
            for i in range(n):
                entries.append(state)
                at = slice(i * edge, (i + 1) * edge)
                state = decay[-1][at] * state + offset[-1][at]
            start = jnp.concatenate(entries, axis=0)
        else:
            own_recv[...] = decay[-1].reshape(n, edge, cols)
            side_recv[...] = offset[-1].reshape(n, edge, cols)

            def compose(i, state):
                entry[i] = state
                return own_recv[i] * state + side_recv[i]

            lax.fori_loop(0, n, compose, jnp.zeros((edge, cols), F32))
            start = entry[...].reshape(count, cols)
        states = [decay[p] * start + offset[p] for p in range(PD)]
        states = jnp.concatenate(
            [
                jnp.where(lower, states[p], pltpu.roll(states[p + 1], cols // 2, 1))
                for p in range(0, PD, 2)
            ],
            axis=1,
        )
        high = states.astype(jnp.bfloat16)
        low = (states - high.astype(F32)).astype(jnp.bfloat16)
        scores = jnp.dot(low, out_high, preferred_element_type=F32) + jnp.dot(
            high, out_low, preferred_element_type=F32
        )
        scores = scores + jnp.dot(high, out_high, preferred_element_type=F32)
        scores = scores.reshape(n, edge, cols)

        def over_planes(x, combine):
            x = combine(x, pltpu.roll(x, rows, 1))
            return combine(x, pltpu.roll(x, 2 * rows, 1))

        highest = over_planes(jnp.max(scores, axis=0), jnp.maximum)
        weights = jnp.exp(scores - highest[None])
        total = over_planes(jnp.sum(weights, axis=0), jnp.add)
        shape = (n, edge, cols)
        plane = lax.rem(lax.broadcasted_iota(I32, shape, 2), PD * rows) // rows
        plane = (plane + PD * lax.broadcasted_iota(I32, shape, 0)).astype(F32)
        value = 1.0 / (0.1 + 0.9 * plane / (PD * n - 1))
        depth = over_planes(jnp.sum(weights * value, axis=0), jnp.add) / total
        block = lax.broadcasted_iota(I32, shape, 2) // (PD * rows)
        column = lax.broadcasted_iota(I32, shape, 1)
        chosen = jnp.where(block == column, weights / total[None], 0.0)
        chosen = jnp.where(block == column + edge, depth[None], chosen)
        fin_send[...] = jnp.sum(chosen, axis=1, keepdims=True)
        fin_own = pltpu.make_async_copy(fin_send.at[me], fin_recv.at[me], smem_sems.at[1])
        fin_own.start()

        def send_fin(k, carry):
            to = far(k)
            push(fin_send.at[to], fin_recv.at[me], {"depth": to}, 4).start()
            return carry

        lax.fori_loop(0, n - 1, send_fin, 0, unroll=once)
        fin_own.wait()
        drain(fin_recv, holders - 1, 4, recv_sems)

    hold() if n == holders else pl.when(me < holders)(hold)
    if n != holders:
        @pl.when(me >= holders)
        def _():
            drain(fin_recv, holders, 4, recv_sems)

    drain(tab_send, n - 1, 0, send_sems)
    drain(code_send, code_rows * (n - 1), 1, send_sems)
    drain(scale_send, n - 1, 5, send_sems)
    drain(side_send, holders, 3, send_sems)
    if n == holders:
        drain(own_send, n - 1, 2, send_sems)
        drain(fin_send, n - 1, 4, send_sems)
    else:
        @pl.when(me < holders)
        def _():
            drain(own_send, holders - 1, 2, send_sems)
            drain(fin_send, n - 1, 4, send_sems)

        @pl.when(me >= holders)
        def _():
            drain(own_send, holders, 2, send_sems)


def hand_over(fin_ref, prob_ref, depth_ref):
    planes, rows, cols = prob_ref.shape
    holders = fin_ref.shape[0]
    edge = cols // holders
    values = jnp.broadcast_to(fin_ref[...], (holders, edge, cols)).reshape(cols, cols)
    block = lax.broadcasted_iota(I32, (cols, cols), 1) // (planes * rows)
    column = lax.broadcasted_iota(I32, (cols, cols), 0)
    values = jnp.where(lax.rem(block, edge) == lax.rem(column, edge), values, 0.0)
    turned = jnp.transpose(values)
    half = cols // 2
    result = turned[:half].reshape(edge, planes * rows, cols).sum(axis=0)
    depth = turned[half:].reshape(edge, planes * rows, cols).sum(axis=0)
    for r in range(rows):
        depth_ref[r : r + 1, :] = depth[r : r + 1]
        for p in range(planes):
            prob_ref[p, r : r + 1, :] = result[p * rows + r : p * rows + r + 1]


def body(ref_feat, src_feat, tile_owner, tile_local, col_shift, w_gates, bias_z, bias_c, w_out):
    n = lax.axis_size("depth")
    rows, feat, cols = ref_feat.shape
    groups = w_gates.shape[2]
    hidden = w_gates.shape[1] // 2
    requests = tile_owner.shape[0]
    cap = max(2, (3 * requests + 2 * n - 1) // (2 * n))
    tiles = (n, 8, cols)
    holders = (cols // 8, 8, cols)
    span = PD * rows * hidden
    anywhere = pl.BlockSpec(memory_space=pl.ANY)
    vmem = pl.BlockSpec(memory_space=pltpu.VMEM)
    shapes = (
        jax.ShapeDtypeStruct((PD, rows, cols), F32),
        jax.ShapeDtypeStruct((rows, cols), F32),
    )
    landed = pl.pallas_call(
        functools.partial(kernel, n, cap),
        out_shape=jax.ShapeDtypeStruct((holders[0], 1, cols), F32),
        in_specs=[anywhere] * 9,
        out_specs=anywhere,
        scratch_shapes=[
            pltpu.VMEM(ref_feat.shape, ref_feat.dtype),
            pltpu.VMEM(src_feat.shape, src_feat.dtype),
            pltpu.VMEM((1, requests), I32),
            pltpu.VMEM((1, requests), I32),
            pltpu.VMEM((1, requests), I32),
            pltpu.VMEM((9, groups, 2 * hidden), w_gates.dtype),
            pltpu.VMEM((1, hidden), F32),
            pltpu.VMEM((1, hidden), F32),
            pltpu.VMEM((1, hidden), F32),
            pltpu.VMEM(ref_feat.shape, F32),
            pltpu.VMEM((n, 1, cols), I32),
            pltpu.VMEM((n, 1, cols), I32),
            pltpu.SMEM((n, 1, cols), I32),
            pltpu.VMEM((1, cols), I32),
            pltpu.SMEM((1, cols), I32),
            pltpu.VMEM((2 * cap, feat, cols), F32),
            pltpu.VMEM((n * cap * groups, cols), jnp.int16),
            pltpu.VMEM((n * cap * groups, cols), jnp.int16),
            pltpu.VMEM((n, cap, cols), F32),
            pltpu.VMEM((n, cap, cols), F32),
            pltpu.VMEM((n * cap, groups, cols), F32),
            pltpu.VMEM((3 * cols, 2 * span), F32),
            pltpu.VMEM((3 * cols, 2 * span), jnp.bfloat16),
            pltpu.VMEM(holders, F32),
            pltpu.VMEM(tiles, F32),
            pltpu.VMEM(holders, F32),
            pltpu.VMEM(tiles, F32),
            pltpu.VMEM(tiles, F32),
            pltpu.VMEM((n, 1, cols), F32),
            pltpu.SemaphoreType.DMA((9,)),
            pltpu.SemaphoreType.DMA((2,)),
            pltpu.SemaphoreType.DMA((6,)),
            pltpu.SemaphoreType.DMA((6,)),
        ],
        compiler_params=pltpu.CompilerParams(
            collective_id=0, has_side_effects=True, vmem_limit_bytes=60 * 1024 * 1024
        ),
        cost_estimate=pl.CostEstimate(
            flops=2 * 144 * 64 * 1024, bytes_accessed=src_feat.size * 2, transcendentals=65536
        ),
    )(
        ref_feat, src_feat, tile_owner.reshape(1, requests), tile_local.reshape(1, requests),
        col_shift.reshape(1, requests), jnp.transpose(w_gates, (0, 2, 1)), bias_z.reshape(1, hidden),
        bias_c.reshape(1, hidden), w_out.reshape(1, hidden),
    )
    return pl.pallas_call(
        hand_over,
        out_shape=shapes,
        in_specs=[vmem],
        out_specs=(vmem, vmem),
        compiler_params=pltpu.CompilerParams(vmem_limit_bytes=60 * 1024 * 1024),
    )(landed)


def solution(mesh):
    return jax.shard_map(
        body,
        mesh=mesh,
        in_specs=(
            P("slab", None, None),
            P("depth", None, None),
            P(("depth", "slab"), None),
            P(("depth", "slab")),
            P(("depth", "slab")),
            P(),
            P(),
            P(),
            P(),
        ),
        out_specs=(P("depth", "slab", None), P("slab", None)),
        check_vma=False,
    )
```

```python
import functools

import jax
import jax.numpy as jnp
from jax import lax
from jax.experimental import pallas as pl
from jax.experimental.pallas import tpu as pltpu
from jax.sharding import PartitionSpec as P

VIEWS = 5
PD = 4
MAXSHIFT = 16
MESH = pl.DeviceIdType.MESH
F32 = jnp.float32
I32 = jnp.int32


def kernel(
    n, cap,
    ref_hbm, src_hbm, owner_hbm, local_hbm, shift_hbm, w_hbm, bz_hbm, bc_hbm, wo_hbm,
    fin_recv,
    ref_ref, src, owner_ref, local_ref, shift_ref, w_ref, bz_ref, bc_ref, wo_ref,
    ref_wide, tab_send, tab_recv, tab_s, own_v, own_s, prod, code_send, code_recv,
    scale_send, scale_recv, answers,
    gates_wide, gates, own_send, own_recv, side_send, side_recv, entry, fin_send,
    in_sems, smem_sems, send_sems, recv_sems,
):
    me = lax.axis_index("depth")
    slab = lax.axis_index("slab")
    requests = owner_ref.shape[1]
    rows, feat, cols = ref_ref.shape
    groups = w_ref.shape[1]
    hidden = w_ref.shape[2] // 2
    cpg = feat // groups

    edge = 8
    holders = cols // edge
    once = n <= 16

    def peer(k):
        return lax.rem(me + k, n)

    def far(j):
        step = (j + 1) // 2
        return peer(n // 2 + jnp.where(lax.rem(j, 2) == 1, -step, step))

    pairs = [
        (owner_hbm, owner_ref), (local_hbm, local_ref), (shift_hbm, shift_ref), (ref_hbm, ref_ref),
        (src_hbm, src), (w_hbm, w_ref), (bz_hbm, bz_ref), (bc_hbm, bc_ref), (wo_hbm, wo_ref),
    ]
    loads = [pltpu.make_async_copy(a, b, in_sems.at[i]) for i, (a, b) in enumerate(pairs)]
    for load in loads:
        load.start()
    barrier = pltpu.get_barrier_semaphore()

    def greet(k, carry):
        pl.semaphore_signal(barrier, inc=1, device_id={"depth": peer(k)}, device_id_type=MESH)
        return carry

    def greet_side(k, carry):
        who = {"depth": peer(k), "slab": 1 - slab}
        pl.semaphore_signal(barrier, inc=1, device_id=who, device_id_type=MESH)
        return carry

    lax.fori_loop(1, n, greet, 0, unroll=once)
    lax.fori_loop(0, n, greet_side, 0, unroll=once)

    q_sub = lax.broadcasted_iota(I32, (requests, requests), 0)
    q_lane = lax.broadcasted_iota(I32, (requests, requests), 1)
    diag = q_sub == q_lane
    for load in loads[:3]:
        load.wait()
    owner_row = owner_ref[...]
    owner_col = jnp.sum(
        jnp.where(diag, owner_row, 0).astype(F32), axis=1, keepdims=True
    ).astype(I32)
    local_col = jnp.sum(jnp.where(diag, local_ref[...], 0).astype(F32), axis=1, keepdims=True)
    shift_col = jnp.sum(
        jnp.where(diag, shift_ref[...] + MAXSHIFT, 0).astype(F32), axis=1, keepdims=True
    )
    same = (owner_row == owner_col) & (q_lane < q_sub)
    slot_col = jnp.sum(jnp.where(same, 1.0, 0.0), axis=1, keepdims=True)
    lane = lax.broadcasted_iota(I32, (requests, cols), 1)
    row_col = lax.rem(lax.broadcasted_iota(I32, (requests, cols), 0), rows).astype(F32)
    kind = lane // cap
    value = jnp.where(
        kind == 0, local_col, jnp.where(kind == 1, shift_col, jnp.where(kind == 2, row_col, 0.0))
    )
    value = jnp.where(lax.rem(lane, cap).astype(F32) == slot_col, value, 0.0)
    owner_hot = jnp.where(
        lax.broadcasted_iota(I32, (n, requests), 0) == owner_row, 1.0, 0.0
    )
    table = jnp.dot(
        owner_hot.astype(jnp.bfloat16), value.astype(jnp.bfloat16), preferred_element_type=F32
    ).astype(I32)
    tab_send[:, 0, :] = table
    place_col = owner_col.astype(F32) * cap + slot_col
    wide_diag = lax.broadcasted_iota(I32, (requests, cols), 0) == lane
    own_v[...] = jnp.sum(jnp.where(wide_diag, place_col, 0.0), axis=0, keepdims=True).astype(I32)
    own_copy = pltpu.make_async_copy(own_v, own_s, smem_sems.at[0])
    own_copy.start()

    def push(source, target, who, number):
        return pltpu.make_async_remote_copy(
            src_ref=source, dst_ref=target, send_sem=send_sems.at[number],
            recv_sem=recv_sems.at[number], device_id=who, device_id_type=MESH,
        )

    def drain_part(buffer, count, part, number, sems):
        got = buffer.at[pl.ds(0, count), part]
        pltpu.make_async_copy(got, got, sems.at[number]).wait()

    def drain(buffer, count, number, sems):
        part = buffer.at[pl.ds(0, count)]
        pltpu.make_async_copy(part, part, sems.at[number]).wait()

    pl.semaphore_wait(barrier, 2 * n - 1)

    def send_table(k, carry):
        to = far(k)
        push(tab_send.at[to], tab_recv.at[me], {"depth": to}, 0).start()
        return carry

    lax.fori_loop(0, n - 1, send_table, 0, unroll=once)
    tab_recv[me] = tab_send[me]
    for load in loads[3:5]:
        load.wait()

    def regroup(at):
        return [prod[at, pl.ds(c, groups, stride=cpg), :] for c in range(cpg)]

    for r in range(rows):
        prod[r] = ref_ref[r].astype(F32)
    for r in range(rows):
        ref_wide[r] = jnp.concatenate(regroup(r), axis=0)
    drain(tab_recv, n - 1, 0, recv_sems)
    tab_copy = pltpu.make_async_copy(tab_recv, tab_s, smem_sems.at[1])
    tab_copy.start()
    tab_copy.wait()

    position = lax.broadcasted_iota(I32, (groups, cols), 1)

    top_code = 32767.0

    def correlate(whos):
        slots = [(who, s) for who in whos for s in range(cap)]
        tiles, shifts, picked = [], [], []
        for who, s in slots:
            tiles.append(jnp.clip(tab_s[who, 0, s], 0, src.shape[0] - 1))
            shifts.append(jnp.clip(tab_s[who, 0, cap + s], 0, 2 * MAXSHIFT) - MAXSHIFT)
            picked.append(jnp.clip(tab_s[who, 0, 2 * cap + s], 0, rows - 1))
        for i, tile in enumerate(tiles):
            prod[i] = src[tile].astype(F32)
        wide = [jnp.concatenate(regroup(i), axis=0) for i in range(len(slots))]
        moved = [pltpu.roll(x, lax.rem(y + cols, cols), 1) for x, y in zip(wide, shifts)]
        totals = []
        for i in range(len(slots)):
            terms = moved[i] * ref_wide[picked[i]]
            total = terms[0:groups]
            for c in range(1, cpg):
                total = total + terms[c * groups : (c + 1) * groups]
            source_col = position - shifts[i]
            inside = (source_col >= 0) & (source_col < cols)
            totals.append(jnp.where(inside, total, 0.0))
        return [totals[i * cap : (i + 1) * cap] for i in range(len(whos))]

    code_rows = cap * groups

    def dispatch(to, totals):
        codes = []
        for s, total in enumerate(totals):
            largest = jnp.maximum(jnp.max(jnp.abs(total), axis=0, keepdims=True), 1e-30)
            codes.append(jnp.round(total * (top_code / largest)).astype(I32))
            scale_send[to, s : s + 1, :] = largest * (1.0 / (top_code * VIEWS * cpg))
        at = pl.ds(pl.multiple_of(to * code_rows, code_rows), code_rows)
        code_send[at, :] = jnp.concatenate(codes, axis=0).astype(jnp.int16)
        home = pl.ds(pl.multiple_of(me * code_rows, code_rows), code_rows)
        push(code_send.at[at], code_recv.at[home], {"depth": to}, 1).start()
        push(scale_send.at[to], scale_recv.at[me], {"depth": to}, 5).start()

    def answer(k, carry):
        pair = [far(2 * k), far(2 * k + 1)]
        for to, totals in zip(pair, correlate(pair)):
            dispatch(to, totals)
        return carry

    lax.fori_loop(0, (n - 1) // 2, answer, 0)
    last = far(n - 2)
    for_last, for_me = correlate([last, me])
    dispatch(last, for_last)
    for s in range(cap):
        answers[me * cap + s] = for_me[s] * (1.0 / (VIEWS * cpg))
    for load in loads[5:]:
        load.wait()
    taps = [w_ref[t].astype(F32) for t in range(9)]
    span = PD * rows * hidden
    plane_of = lax.broadcasted_iota(I32, (groups, span), 1) // (rows * hidden)

    def fill(at, pieces):
        for kind in range(2):
            units = slice(kind * hidden, (kind + 1) * hidden)
            part = jnp.concatenate([x[:, units] for x in pieces] * PD, axis=1)
            for p in range(PD):
                gates_wide[pl.ds(at(p), groups), pl.ds(kind * span, span)] = jnp.where(
                    plane_of == p, part, 0.0
                )

    own_rows = PD * rows * groups
    for b in range(3):
        for r in range(rows):
            fill(
                lambda p: b * cols + (p * rows + r) * groups,
                [taps[(r - to + 1) * 3 + b] for to in range(rows)],
            )
        pieces = [jnp.zeros((groups, 2 * hidden), F32) for _ in range(rows)]
        pieces[0] = pieces[0] + jnp.where(slab == 1, taps[b], 0.0)
        pieces[-1] = pieces[-1] + jnp.where(slab == 0, taps[6 + b], 0.0)
        fill(lambda p: b * cols + own_rows + p * groups, pieces)
        rest = own_rows + PD * groups
        gates_wide[pl.ds(b * cols + rest, cols - rest), :] = jnp.zeros((cols - rest, 2 * span), F32)
    gates[...] = gates_wide[...].astype(jnp.bfloat16)
    bias_z = jnp.concatenate([bz_ref[...]] * (PD * rows), axis=1)
    bias_c = jnp.concatenate([bc_ref[...]] * (PD * rows), axis=1)
    h_eye = lax.broadcasted_iota(I32, (hidden, hidden), 0) == lax.broadcasted_iota(
        I32, (hidden, hidden), 1
    )
    out_col = jnp.sum(jnp.where(h_eye, wo_ref[...], 0.0), axis=1, keepdims=True)
    out_col = jnp.concatenate([out_col] * (PD * rows), axis=0)
    unit_block = lax.broadcasted_iota(I32, (span, cols), 0) // hidden
    lane_block = lax.rem(lax.broadcasted_iota(I32, (span, cols), 1), PD * rows)
    out_wide = jnp.where(unit_block == lane_block, out_col, 0.0)
    out_high = out_wide.astype(jnp.bfloat16)
    out_low = (out_wide - out_high.astype(F32)).astype(jnp.bfloat16)
    own_copy.wait()
    drain(code_recv, code_rows * (n - 1), 1, recv_sems)
    drain(scale_recv, n - 1, 5, recv_sems)

    def decode(k, carry):
        source = peer(k)
        at = pl.ds(pl.multiple_of(source * code_rows, code_rows), code_rows)
        values = code_recv[at, :].astype(I32).astype(F32)
        for s in range(cap):
            part = values[s * groups : (s + 1) * groups]
            answers[source * cap + s] = part * scale_recv[source, s : s + 1, :]
        return carry

    lax.fori_loop(1, n, decode, 0, unroll=once)
    cost = {}
    for p in range(PD):
        for r in range(rows):
            total = None
            for v in range(VIEWS):
                place = jnp.clip(own_s[0, (p * VIEWS + v) * rows + r], 0, n * cap - 1)
                term = answers[place]
                total = term if total is None else total + term
            cost[p, r] = total

    in_block = lax.rem(position, edge)

    def turned(x, by):
        moved = pltpu.roll(x, by % cols, 1)
        return jnp.where((position >= by) & (position < cols + by), moved, 0.0)

    blocks = [cost[p, r] for p in range(PD) for r in range(rows)]
    near = [jnp.where(slab == 0, cost[p, rows - 1], cost[p, 0]) for p in range(PD)]
    side = [jnp.where(in_block < 2, x, turned(x, 3)) for x in near]
    side += [jnp.where(in_block < 2, turned(x, -2), turned(x, -6)) for x in near]
    side += [turned(x, -4) for x in near] + [turned(x, -6) for x in near]
    side = jnp.concatenate(side, axis=0)
    side_send[...] = jnp.transpose(side).reshape(holders, edge, cols)
    own_part, side_part = pl.ds(0, 5), pl.ds(0, 3)

    def send_side(k, carry):
        to = far(k) if n == holders else k
        who = {"depth": to, "slab": 1 - slab}
        push(side_send.at[to, side_part], side_recv.at[me, side_part], who, 3).start()
        return carry

    own = [jnp.where(in_block < 4, x, turned(x, 5)) for x in blocks]
    own = jnp.concatenate(own + [turned(x, -4) for x in blocks], axis=0)
    own_send[...] = jnp.transpose(own).reshape(holders, edge, cols)

    def send_own(k, carry):
        to = far(k) if n == holders else k

        def go():
            push(
                own_send.at[to, own_part], own_recv.at[me, own_part], {"depth": to}, 2
            ).start()

        go() if n == holders else pl.when(to != me)(go)
        return carry

    if n == holders:
        def send_both(k, carry):
            send_own(k, carry)
            return send_side(k, carry)

        lax.fori_loop(0, n - 1, send_both, 0, unroll=once)
        send_side_me = {"depth": me, "slab": 1 - slab}
        push(side_send.at[me, side_part], side_recv.at[me, side_part], send_side_me, 3).start()
    else:
        lax.fori_loop(0, holders, send_own, 0)
        lax.fori_loop(0, holders, send_side, 0)

    def hold():
        own_recv[me] = own_send[me]
        drain_part(own_recv, n - 1, own_part, 2, recv_sems)
        drain_part(side_recv, n, side_part, 3, recv_sems)
        count = n * edge
        here = own_recv[...].reshape(count, cols)
        beside = side_recv[...].reshape(count, cols)
        lane = lax.broadcasted_iota(I32, (count, cols), 1)
        place = lax.rem(lax.broadcasted_iota(I32, (count, cols), 0), edge)
        lower = lane < cols // 2

        def down(x, by):
            return pltpu.roll(x, by % count, 0)

        here_2 = pltpu.roll(here, cols // 2, 1)
        quarter = [pltpu.roll(beside, (64 - 32 * q) % cols, 1) if q != 2 else beside for q in range(4)]
        main_1 = jnp.where(place < 4, here, down(here_2, 4))
        main_2 = quarter[0]
        for q in range(1, 4):
            main_2 = jnp.where(place >= 2 * q, down(quarter[q], 2 * q), main_2)
        main = jnp.where(lower, main_1, main_2)
        first = jnp.where(lower, down(here, -4), down(quarter[0], -2))
        final = jnp.where(lower, down(here_2, 3), down(quarter[1], 5))
        before = jnp.where(place == 0, first, down(main, 1))
        after = jnp.where(place == edge - 1, final, down(main, -1))
        live = lane < cols // 2 + PD * groups
        before, main, after = [jnp.where(live, x, 0.0) for x in (before, main, after)]
        window = jnp.concatenate([before, main, after], axis=1)
        high = window.astype(jnp.bfloat16)
        low = (window - high.astype(F32)).astype(jnp.bfloat16)
        both = jnp.dot(
            jnp.concatenate([high, low], axis=0), gates[...], preferred_element_type=F32
        )
        preact = both[:count] + both[count:]
        retain = jax.nn.sigmoid(preact[:, :span] + bias_z)
        fresh = (1.0 - retain) * jnp.tanh(preact[:, span:] + bias_c)

        def planes(x):
            pair = [x[:, :cols], x[:, cols:]]
            return [pair[0], pltpu.roll(pair[0], cols // 2, 1), pair[1], pltpu.roll(pair[1], cols // 2, 1)]

        keep, new = planes(retain), planes(fresh)
        decay, offset = [keep[0]], [new[0]]
        for p in range(1, PD):
            decay.append(keep[p] * decay[-1])
            offset.append(keep[p] * offset[-1] + new[p])
        if once:
            state, entries = jnp.zeros((edge, cols), F32), []
            for i in range(n):
                entries.append(state)
                at = slice(i * edge, (i + 1) * edge)
                state = decay[-1][at] * state + offset[-1][at]
            start = jnp.concatenate(entries, axis=0)
        else:
            own_recv[...] = decay[-1].reshape(n, edge, cols)
            side_recv[...] = offset[-1].reshape(n, edge, cols)

            def compose(i, state):
                entry[i] = state
                return own_recv[i] * state + side_recv[i]

            lax.fori_loop(0, n, compose, jnp.zeros((edge, cols), F32))
            start = entry[...].reshape(count, cols)
        states = [decay[p] * start + offset[p] for p in range(PD)]
        states = jnp.concatenate(
            [
                jnp.where(lower, states[p], pltpu.roll(states[p + 1], cols // 2, 1))
                for p in range(0, PD, 2)
            ],
            axis=1,
        )
        high = states.astype(jnp.bfloat16)
        low = (states - high.astype(F32)).astype(jnp.bfloat16)
        scores = jnp.dot(low, out_high, preferred_element_type=F32) + jnp.dot(
            high, out_low, preferred_element_type=F32
        )
        scores = scores + jnp.dot(high, out_high, preferred_element_type=F32)
        scores = scores.reshape(n, edge, cols)

        def over_planes(x, combine):
            x = combine(x, pltpu.roll(x, rows, 1))
            return combine(x, pltpu.roll(x, 2 * rows, 1))

        highest = over_planes(jnp.max(scores, axis=0), jnp.maximum)
        weights = jnp.exp(scores - highest[None])
        total = over_planes(jnp.sum(weights, axis=0), jnp.add)
        shape = (n, edge, cols)
        plane = lax.rem(lax.broadcasted_iota(I32, shape, 2), PD * rows) // rows
        plane = (plane + PD * lax.broadcasted_iota(I32, shape, 0)).astype(F32)
        value = 1.0 / (0.1 + 0.9 * plane / (PD * n - 1))
        depth = over_planes(jnp.sum(weights * value, axis=0), jnp.add) / total
        block = lax.broadcasted_iota(I32, shape, 2) // (PD * rows)
        column = lax.broadcasted_iota(I32, shape, 1)
        chosen = jnp.where(block == column, weights / total[None], 0.0)
        chosen = jnp.where(block == column + edge, depth[None], chosen)
        fin_send[...] = jnp.sum(chosen, axis=1, keepdims=True)
        fin_own = pltpu.make_async_copy(fin_send.at[me], fin_recv.at[me], smem_sems.at[1])
        fin_own.start()

        def send_fin(k, carry):
            to = far(k)
            push(fin_send.at[to], fin_recv.at[me], {"depth": to}, 4).start()
            return carry

        lax.fori_loop(0, n - 1, send_fin, 0, unroll=once)
        fin_own.wait()
        drain(fin_recv, holders - 1, 4, recv_sems)

    hold() if n == holders else pl.when(me < holders)(hold)
    if n != holders:
        @pl.when(me >= holders)
        def _():
            drain(fin_recv, holders, 4, recv_sems)

    drain(tab_send, n - 1, 0, send_sems)
    drain(code_send, code_rows * (n - 1), 1, send_sems)
    drain(scale_send, n - 1, 5, send_sems)
    drain_part(side_send, holders, side_part, 3, send_sems)
    if n == holders:
        drain_part(own_send, n - 1, own_part, 2, send_sems)
        drain(fin_send, n - 1, 4, send_sems)
    else:
        @pl.when(me < holders)
        def _():
            drain_part(own_send, holders - 1, own_part, 2, send_sems)
            drain(fin_send, n - 1, 4, send_sems)

        @pl.when(me >= holders)
        def _():
            drain_part(own_send, holders, own_part, 2, send_sems)


def hand_over(fin_ref, prob_ref, depth_ref):
    planes, rows, cols = prob_ref.shape
    holders = fin_ref.shape[0]
    edge = cols // holders
    values = jnp.broadcast_to(fin_ref[...], (holders, edge, cols)).reshape(cols, cols)
    block = lax.broadcasted_iota(I32, (cols, cols), 1) // (planes * rows)
    column = lax.broadcasted_iota(I32, (cols, cols), 0)
    values = jnp.where(lax.rem(block, edge) == lax.rem(column, edge), values, 0.0)
    turned = jnp.transpose(values)
    half = cols // 2
    result = turned[:half].reshape(edge, planes * rows, cols).sum(axis=0)
    depth = turned[half:].reshape(edge, planes * rows, cols).sum(axis=0)
    for r in range(rows):
        depth_ref[r : r + 1, :] = depth[r : r + 1]
        for p in range(planes):
            prob_ref[p, r : r + 1, :] = result[p * rows + r : p * rows + r + 1]


def body(ref_feat, src_feat, tile_owner, tile_local, col_shift, w_gates, bias_z, bias_c, w_out):
    n = lax.axis_size("depth")
    rows, feat, cols = ref_feat.shape
    groups = w_gates.shape[2]
    hidden = w_gates.shape[1] // 2
    requests = tile_owner.shape[0]
    cap = max(2, (3 * requests + 2 * n - 1) // (2 * n))
    tiles = (n, 8, cols)
    holders = (cols // 8, 8, cols)
    span = PD * rows * hidden
    anywhere = pl.BlockSpec(memory_space=pl.ANY)
    vmem = pl.BlockSpec(memory_space=pltpu.VMEM)
    shapes = (
        jax.ShapeDtypeStruct((PD, rows, cols), F32),
        jax.ShapeDtypeStruct((rows, cols), F32),
    )
    landed = pl.pallas_call(
        functools.partial(kernel, n, cap),
        out_shape=jax.ShapeDtypeStruct((holders[0], 1, cols), F32),
        in_specs=[anywhere] * 9,
        out_specs=anywhere,
        scratch_shapes=[
            pltpu.VMEM(ref_feat.shape, ref_feat.dtype),
            pltpu.VMEM(src_feat.shape, src_feat.dtype),
            pltpu.VMEM((1, requests), I32),
            pltpu.VMEM((1, requests), I32),
            pltpu.VMEM((1, requests), I32),
            pltpu.VMEM((9, groups, 2 * hidden), w_gates.dtype),
            pltpu.VMEM((1, hidden), F32),
            pltpu.VMEM((1, hidden), F32),
            pltpu.VMEM((1, hidden), F32),
            pltpu.VMEM(ref_feat.shape, F32),
            pltpu.VMEM((n, 1, cols), I32),
            pltpu.VMEM((n, 1, cols), I32),
            pltpu.SMEM((n, 1, cols), I32),
            pltpu.VMEM((1, cols), I32),
            pltpu.SMEM((1, cols), I32),
            pltpu.VMEM((2 * cap, feat, cols), F32),
            pltpu.VMEM((n * cap * groups, cols), jnp.int16),
            pltpu.VMEM((n * cap * groups, cols), jnp.int16),
            pltpu.VMEM((n, cap, cols), F32),
            pltpu.VMEM((n, cap, cols), F32),
            pltpu.VMEM((n * cap, groups, cols), F32),
            pltpu.VMEM((3 * cols, 2 * span), F32),
            pltpu.VMEM((3 * cols, 2 * span), jnp.bfloat16),
            pltpu.VMEM(holders, F32),
            pltpu.VMEM(tiles, F32),
            pltpu.VMEM(holders, F32),
            pltpu.VMEM(tiles, F32),
            pltpu.VMEM(tiles, F32),
            pltpu.VMEM((n, 1, cols), F32),
            pltpu.SemaphoreType.DMA((9,)),
            pltpu.SemaphoreType.DMA((2,)),
            pltpu.SemaphoreType.DMA((6,)),
            pltpu.SemaphoreType.DMA((6,)),
        ],
        compiler_params=pltpu.CompilerParams(
            collective_id=0, has_side_effects=True, vmem_limit_bytes=60 * 1024 * 1024
        ),
        cost_estimate=pl.CostEstimate(
            flops=2 * 144 * 64 * 1024, bytes_accessed=src_feat.size * 2, transcendentals=65536
        ),
    )(
        ref_feat, src_feat, tile_owner.reshape(1, requests), tile_local.reshape(1, requests),
        col_shift.reshape(1, requests), jnp.transpose(w_gates, (0, 2, 1)), bias_z.reshape(1, hidden),
        bias_c.reshape(1, hidden), w_out.reshape(1, hidden),
    )
    return pl.pallas_call(
        hand_over,
        out_shape=shapes,
        in_specs=[vmem],
        out_specs=(vmem, vmem),
        compiler_params=pltpu.CompilerParams(vmem_limit_bytes=60 * 1024 * 1024),
    )(landed)


def solution(mesh):
    return jax.shard_map(
        body,
        mesh=mesh,
        in_specs=(
            P("slab", None, None),
            P("depth", None, None),
            P(("depth", "slab"), None),
            P(("depth", "slab")),
            P(("depth", "slab")),
            P(),
            P(),
            P(),
            P(),
        ),
        out_specs=(P("depth", "slab", None), P("slab", None)),
        check_vma=False,
    )
```

```python
import functools

import jax
import jax.numpy as jnp
from jax import lax
from jax.experimental import pallas as pl
from jax.experimental.pallas import tpu as pltpu
from jax.sharding import PartitionSpec as P

VIEWS = 5
PD = 4
MAXSHIFT = 16
MESH = pl.DeviceIdType.MESH
F32 = jnp.float32
I32 = jnp.int32


def kernel(
    n, cap,
    ref_hbm, src_hbm, owner_hbm, local_hbm, shift_hbm, w_hbm, bz_hbm, bc_hbm, wo_hbm,
    fin_recv,
    ref_ref, src, owner_ref, local_ref, shift_ref, w_ref, bz_ref, bc_ref, wo_ref,
    ref_wide, tab_send, tab_recv, tab_s, own_v, own_s, prod, code_send, code_recv,
    scale_send, scale_recv, answers,
    gates_wide, gates, own_send, own_recv, side_send, side_recv, entry, fin_send,
    in_sems, smem_sems, send_sems, recv_sems,
):
    me = lax.axis_index("depth")
    slab = lax.axis_index("slab")
    requests = owner_ref.shape[1]
    rows, feat, cols = ref_ref.shape
    groups = w_ref.shape[1]
    hidden = w_ref.shape[2] // 2
    cpg = feat // groups

    edge = 8
    holders = cols // edge
    once = n <= 16

    def peer(k):
        return lax.rem(me + k, n)

    def far(j):
        step = (j + 1) // 2
        return peer(n // 2 + jnp.where(lax.rem(j, 2) == 1, -step, step))

    pairs = [
        (owner_hbm, owner_ref), (local_hbm, local_ref), (shift_hbm, shift_ref), (ref_hbm, ref_ref),
        (src_hbm, src), (w_hbm, w_ref), (bz_hbm, bz_ref), (bc_hbm, bc_ref), (wo_hbm, wo_ref),
    ]
    loads = [pltpu.make_async_copy(a, b, in_sems.at[i]) for i, (a, b) in enumerate(pairs)]
    for load in loads:
        load.start()
    barrier = pltpu.get_barrier_semaphore()

    def greet(k, carry):
        pl.semaphore_signal(barrier, inc=1, device_id={"depth": peer(k)}, device_id_type=MESH)
        return carry

    def greet_side(k, carry):
        who = {"depth": peer(k), "slab": 1 - slab}
        pl.semaphore_signal(barrier, inc=1, device_id=who, device_id_type=MESH)
        return carry

    lax.fori_loop(1, n, greet, 0, unroll=once)
    lax.fori_loop(0, n, greet_side, 0, unroll=once)

    q_sub = lax.broadcasted_iota(I32, (requests, requests), 0)
    q_lane = lax.broadcasted_iota(I32, (requests, requests), 1)
    diag = q_sub == q_lane
    for load in loads[:3]:
        load.wait()
    owner_row = owner_ref[...]
    owner_col = jnp.sum(
        jnp.where(diag, owner_row, 0).astype(F32), axis=1, keepdims=True
    ).astype(I32)
    local_col = jnp.sum(jnp.where(diag, local_ref[...], 0).astype(F32), axis=1, keepdims=True)
    shift_col = jnp.sum(
        jnp.where(diag, shift_ref[...] + MAXSHIFT, 0).astype(F32), axis=1, keepdims=True
    )
    same = (owner_row == owner_col) & (q_lane < q_sub)
    slot_col = jnp.sum(jnp.where(same, 1.0, 0.0), axis=1, keepdims=True)
    lane = lax.broadcasted_iota(I32, (requests, cols), 1)
    row_col = lax.rem(lax.broadcasted_iota(I32, (requests, cols), 0), rows).astype(F32)
    kind = lane // cap
    value = jnp.where(
        kind == 0, local_col, jnp.where(kind == 1, shift_col, jnp.where(kind == 2, row_col, 0.0))
    )
    value = jnp.where(lax.rem(lane, cap).astype(F32) == slot_col, value, 0.0)
    owner_hot = jnp.where(
        lax.broadcasted_iota(I32, (n, requests), 0) == owner_row, 1.0, 0.0
    )
    table = jnp.dot(
        owner_hot.astype(jnp.bfloat16), value.astype(jnp.bfloat16), preferred_element_type=F32
    ).astype(I32)
    tab_send[:, 0, :] = table
    place_col = owner_col.astype(F32) * cap + slot_col
    wide_diag = lax.broadcasted_iota(I32, (requests, cols), 0) == lane
    own_v[...] = jnp.sum(jnp.where(wide_diag, place_col, 0.0), axis=0, keepdims=True).astype(I32)
    own_copy = pltpu.make_async_copy(own_v, own_s, smem_sems.at[0])
    own_copy.start()

    def push(source, target, who, number):
        return pltpu.make_async_remote_copy(
            src_ref=source, dst_ref=target, send_sem=send_sems.at[number],
            recv_sem=recv_sems.at[number], device_id=who, device_id_type=MESH,
        )

    def drain_part(buffer, count, part, number, sems):
        got = buffer.at[pl.ds(0, count), part]
        pltpu.make_async_copy(got, got, sems.at[number]).wait()

    def drain(buffer, count, number, sems):
        part = buffer.at[pl.ds(0, count)]
        pltpu.make_async_copy(part, part, sems.at[number]).wait()

    pl.semaphore_wait(barrier, 2 * n - 1)

    def send_table(k, carry):
        to = far(k)
        push(tab_send.at[to], tab_recv.at[me], {"depth": to}, 0).start()
        return carry

    lax.fori_loop(0, n - 1, send_table, 0, unroll=once)
    tab_recv[me] = tab_send[me]
    for load in loads[3:5]:
        load.wait()

    def regroup(at):
        return [prod[at, pl.ds(c, groups, stride=cpg), :] for c in range(cpg)]

    for r in range(rows):
        prod[r] = ref_ref[r].astype(F32)
    for r in range(rows):
        ref_wide[r] = jnp.concatenate(regroup(r), axis=0)
    drain(tab_recv, n - 1, 0, recv_sems)
    tab_copy = pltpu.make_async_copy(tab_recv, tab_s, smem_sems.at[1])
    tab_copy.start()
    tab_copy.wait()

    position = lax.broadcasted_iota(I32, (groups, cols), 1)

    top_code = 32767.0

    def correlate(whos):
        slots = [(who, s) for who in whos for s in range(cap)]
        tiles, shifts, picked = [], [], []
        for who, s in slots:
            tiles.append(jnp.clip(tab_s[who, 0, s], 0, src.shape[0] - 1))
            shifts.append(jnp.clip(tab_s[who, 0, cap + s], 0, 2 * MAXSHIFT) - MAXSHIFT)
            picked.append(jnp.clip(tab_s[who, 0, 2 * cap + s], 0, rows - 1))
        for i, tile in enumerate(tiles):
            prod[i] = src[tile].astype(F32)
        wide = [jnp.concatenate(regroup(i), axis=0) for i in range(len(slots))]
        moved = [pltpu.roll(x, lax.rem(y + cols, cols), 1) for x, y in zip(wide, shifts)]
        totals = []
        for i in range(len(slots)):
            terms = moved[i] * ref_wide[picked[i]]
            total = terms[0:groups]
            for c in range(1, cpg):
                total = total + terms[c * groups : (c + 1) * groups]
            source_col = position - shifts[i]
            inside = (source_col >= 0) & (source_col < cols)
            totals.append(jnp.where(inside, total, 0.0))
        return [totals[i * cap : (i + 1) * cap] for i in range(len(whos))]

    code_rows = cap * groups

    def dispatch(to, totals):
        codes = []
        for s, total in enumerate(totals):
            largest = jnp.maximum(jnp.max(jnp.abs(total), axis=0, keepdims=True), 1e-30)
            codes.append(jnp.round(total * (top_code / largest)).astype(I32))
            scale_send[to, s : s + 1, :] = largest * (1.0 / (top_code * VIEWS * cpg))
        at = pl.ds(pl.multiple_of(to * code_rows, code_rows), code_rows)
        code_send[at, :] = jnp.concatenate(codes, axis=0).astype(jnp.int16)
        home = pl.ds(pl.multiple_of(me * code_rows, code_rows), code_rows)
        push(code_send.at[at], code_recv.at[home], {"depth": to}, 1).start()
        push(scale_send.at[to], scale_recv.at[me], {"depth": to}, 5).start()

    def answer(k, carry):
        pair = [far(2 * k), far(2 * k + 1)]
        for to, totals in zip(pair, correlate(pair)):
            dispatch(to, totals)
        return carry

    lax.fori_loop(0, (n - 1) // 2, answer, 0)
    last = far(n - 2)
    for_last, for_me = correlate([last, me])
    dispatch(last, for_last)
    for s in range(cap):
        answers[me * cap + s] = for_me[s] * (1.0 / (VIEWS * cpg))
    for load in loads[5:]:
        load.wait()
    taps = [w_ref[t].astype(F32) for t in range(9)]
    span = PD * rows * hidden
    plane_of = lax.broadcasted_iota(I32, (groups, span), 1) // (rows * hidden)

    def fill(at, pieces):
        for kind in range(2):
            units = slice(kind * hidden, (kind + 1) * hidden)
            part = jnp.concatenate([x[:, units] for x in pieces] * PD, axis=1)
            for p in range(PD):
                gates_wide[pl.ds(at(p), groups), pl.ds(kind * span, span)] = jnp.where(
                    plane_of == p, part, 0.0
                )

    own_rows = PD * rows * groups
    for b in range(3):
        for r in range(rows):
            fill(
                lambda p: b * cols + (p * rows + r) * groups,
                [taps[(r - to + 1) * 3 + b] for to in range(rows)],
            )
        pieces = [jnp.zeros((groups, 2 * hidden), F32) for _ in range(rows)]
        pieces[0] = pieces[0] + jnp.where(slab == 1, taps[b], 0.0)
        pieces[-1] = pieces[-1] + jnp.where(slab == 0, taps[6 + b], 0.0)
        fill(lambda p: b * cols + own_rows + p * groups, pieces)
        rest = own_rows + PD * groups
        gates_wide[pl.ds(b * cols + rest, cols - rest), :] = jnp.zeros((cols - rest, 2 * span), F32)
    gates[...] = gates_wide[...].astype(jnp.bfloat16)
    bias_z = jnp.concatenate([bz_ref[...]] * (PD * rows), axis=1)
    bias_c = jnp.concatenate([bc_ref[...]] * (PD * rows), axis=1)
    h_eye = lax.broadcasted_iota(I32, (hidden, hidden), 0) == lax.broadcasted_iota(
        I32, (hidden, hidden), 1
    )
    out_col = jnp.sum(jnp.where(h_eye, wo_ref[...], 0.0), axis=1, keepdims=True)
    out_col = jnp.concatenate([out_col] * (PD * rows), axis=0)
    unit_block = lax.broadcasted_iota(I32, (span, cols), 0) // hidden
    lane_block = lax.rem(lax.broadcasted_iota(I32, (span, cols), 1), PD * rows)
    out_wide = jnp.where(unit_block == lane_block, out_col, 0.0)
    out_high = out_wide.astype(jnp.bfloat16)
    out_low = (out_wide - out_high.astype(F32)).astype(jnp.bfloat16)
    own_copy.wait()
    drain(code_recv, code_rows * (n - 1), 1, recv_sems)
    drain(scale_recv, n - 1, 5, recv_sems)

    def decode(k, carry):
        source = peer(k)
        at = pl.ds(pl.multiple_of(source * code_rows, code_rows), code_rows)
        values = code_recv[at, :].astype(I32).astype(F32)
        for s in range(cap):
            part = values[s * groups : (s + 1) * groups]
            answers[source * cap + s] = part * scale_recv[source, s : s + 1, :]
        return carry

    lax.fori_loop(1, n, decode, 0, unroll=once)
    cost = {}
    for p in range(PD):
        for r in range(rows):
            total = None
            for v in range(VIEWS):
                place = jnp.clip(own_s[0, (p * VIEWS + v) * rows + r], 0, n * cap - 1)
                term = answers[place]
                total = term if total is None else total + term
            cost[p, r] = total

    in_block = lax.rem(position, edge)

    def turned(x, by):
        moved = pltpu.roll(x, by % cols, 1)
        return jnp.where((position >= by) & (position < cols + by), moved, 0.0)

    blocks = [cost[p, r] for p in range(PD) for r in range(rows)]
    near = [jnp.where(slab == 0, cost[p, rows - 1], cost[p, 0]) for p in range(PD)]
    side = [jnp.where(in_block < 2, x, turned(x, 3)) for x in near]
    side += [jnp.where(in_block < 2, turned(x, -2), turned(x, -6)) for x in near]
    side += [turned(x, -4) for x in near] + [turned(x, -6) for x in near]
    side = jnp.concatenate(side, axis=0)
    side_send[...] = jnp.transpose(side).reshape(holders, edge, cols)
    own_part, side_part = pl.ds(0, 5), pl.ds(0, 3)

    def send_side(k, carry):
        to = far(k) if n == holders else k
        who = {"depth": to, "slab": 1 - slab}
        push(side_send.at[to, side_part], side_recv.at[me, side_part], who, 3).start()
        return carry

    own = [jnp.where(in_block < 4, x, turned(x, 5)) for x in blocks]
    own = jnp.concatenate(own + [turned(x, -4) for x in blocks], axis=0)
    own_send[...] = jnp.transpose(own).reshape(holders, edge, cols)

    def send_own(k, carry):
        to = far(k) if n == holders else k

        def go():
            push(
                own_send.at[to, own_part], own_recv.at[me, own_part], {"depth": to}, 2
            ).start()

        go() if n == holders else pl.when(to != me)(go)
        return carry

    if n == holders:
        def send_both(k, carry):
            send_own(k, carry)
            return send_side(k, carry)

        lax.fori_loop(0, n - 1, send_both, 0, unroll=once)
        send_side_me = {"depth": me, "slab": 1 - slab}
        push(side_send.at[me, side_part], side_recv.at[me, side_part], send_side_me, 3).start()
    else:
        lax.fori_loop(0, holders, send_own, 0)
        lax.fori_loop(0, holders, send_side, 0)

    def hold():
        own_recv[me] = own_send[me]
        drain_part(own_recv, n - 1, own_part, 2, recv_sems)
        drain_part(side_recv, n, side_part, 3, recv_sems)
        count = n * edge
        here = own_recv[...].reshape(count, cols)
        beside = side_recv[...].reshape(count, cols)
        lane = lax.broadcasted_iota(I32, (count, cols), 1)
        place = lax.rem(lax.broadcasted_iota(I32, (count, cols), 0), edge)
        lower = lane < cols // 2

        def down(x, by):
            return pltpu.roll(x, by % count, 0)

        here_2 = pltpu.roll(here, cols // 2, 1)
        quarter = [pltpu.roll(beside, (64 - 32 * q) % cols, 1) if q != 2 else beside for q in range(4)]
        main_1 = jnp.where(place < 4, here, down(here_2, 4))
        main_2 = quarter[0]
        for q in range(1, 4):
            main_2 = jnp.where(place >= 2 * q, down(quarter[q], 2 * q), main_2)
        main = jnp.where(lower, main_1, main_2)
        first = jnp.where(lower, down(here, -4), down(quarter[0], -2))
        final = jnp.where(lower, down(here_2, 3), down(quarter[1], 5))
        before = jnp.where(place == 0, first, down(main, 1))
        after = jnp.where(place == edge - 1, final, down(main, -1))
        live = lane < cols // 2 + PD * groups
        before, main, after = [jnp.where(live, x, 0.0) for x in (before, main, after)]
        window = jnp.concatenate([before, main, after], axis=1)
        high = window.astype(jnp.bfloat16)
        low = (window - high.astype(F32)).astype(jnp.bfloat16)
        both = jnp.dot(
            jnp.concatenate([high, low], axis=0), gates[...], preferred_element_type=F32
        )
        preact = both[:count] + both[count:]
        retain = jax.nn.sigmoid(preact[:, :span] + bias_z)
        fresh = (1.0 - retain) * jnp.tanh(preact[:, span:] + bias_c)

        def planes(x):
            pair = [x[:, :cols], x[:, cols:]]
            return [pair[0], pltpu.roll(pair[0], cols // 2, 1), pair[1], pltpu.roll(pair[1], cols // 2, 1)]

        keep, new = planes(retain), planes(fresh)
        decay, offset = [keep[0]], [new[0]]
        for p in range(1, PD):
            decay.append(keep[p] * decay[-1])
            offset.append(keep[p] * offset[-1] + new[p])
        if once:
            state, entries = jnp.zeros((edge, cols), F32), []
            for i in range(n):
                entries.append(state)
                at = slice(i * edge, (i + 1) * edge)
                state = decay[-1][at] * state + offset[-1][at]
            start = jnp.concatenate(entries, axis=0)
        else:
            own_recv[...] = decay[-1].reshape(n, edge, cols)
            side_recv[...] = offset[-1].reshape(n, edge, cols)

            def compose(i, state):
                entry[i] = state
                return own_recv[i] * state + side_recv[i]

            lax.fori_loop(0, n, compose, jnp.zeros((edge, cols), F32))
            start = entry[...].reshape(count, cols)
        states = [decay[p] * start + offset[p] for p in range(PD)]
        states = jnp.concatenate(
            [
                jnp.where(lower, states[p], pltpu.roll(states[p + 1], cols // 2, 1))
                for p in range(0, PD, 2)
            ],
            axis=1,
        )
        high = states.astype(jnp.bfloat16)
        low = (states - high.astype(F32)).astype(jnp.bfloat16)
        scores = jnp.dot(low, out_high, preferred_element_type=F32) + jnp.dot(
            high, out_low, preferred_element_type=F32
        )
        scores = scores + jnp.dot(high, out_high, preferred_element_type=F32)
        scores = scores.reshape(n, edge, cols)

        def over_planes(x, combine):
            x = combine(x, pltpu.roll(x, rows, 1))
            return combine(x, pltpu.roll(x, 2 * rows, 1))

        highest = over_planes(jnp.max(scores, axis=0), jnp.maximum)
        weights = jnp.exp(scores - highest[None])
        total = over_planes(jnp.sum(weights, axis=0), jnp.add)
        shape = (n, edge, cols)
        plane = lax.rem(lax.broadcasted_iota(I32, shape, 2), PD * rows) // rows
        plane = (plane + PD * lax.broadcasted_iota(I32, shape, 0)).astype(F32)
        value = 1.0 / (0.1 + 0.9 * plane / (PD * n - 1))
        depth = over_planes(jnp.sum(weights * value, axis=0), jnp.add) / total
        block = lax.broadcasted_iota(I32, shape, 2) // (PD * rows)
        column = lax.broadcasted_iota(I32, shape, 1)
        chosen = jnp.where(block == column, weights / total[None], 0.0)
        chosen = jnp.where(block == column + edge, depth[None], chosen)
        fin_send[...] = jnp.sum(chosen, axis=1, keepdims=True)
        fin_own = pltpu.make_async_copy(fin_send.at[me], fin_recv.at[me], smem_sems.at[1])
        fin_own.start()

        def send_fin(k, carry):
            to = far(k)
            push(fin_send.at[to], fin_recv.at[me], {"depth": to}, 4).start()
            return carry

        lax.fori_loop(0, n - 1, send_fin, 0, unroll=once)
        fin_own.wait()
        drain(fin_recv, holders - 1, 4, recv_sems)

    hold() if n == holders else pl.when(me < holders)(hold)
    if n != holders:
        @pl.when(me >= holders)
        def _():
            drain(fin_recv, holders, 4, recv_sems)

    drain(tab_send, n - 1, 0, send_sems)
    drain(code_send, code_rows * (n - 1), 1, send_sems)
    drain(scale_send, n - 1, 5, send_sems)
    drain_part(side_send, holders, side_part, 3, send_sems)
    if n == holders:
        drain_part(own_send, n - 1, own_part, 2, send_sems)
        drain(fin_send, n - 1, 4, send_sems)
    else:
        @pl.when(me < holders)
        def _():
            drain_part(own_send, holders - 1, own_part, 2, send_sems)
            drain(fin_send, n - 1, 4, send_sems)

        @pl.when(me >= holders)
        def _():
            drain_part(own_send, holders, own_part, 2, send_sems)


def hand_over(fin_ref, prob_ref, depth_ref):
    planes, rows, cols = prob_ref.shape
    holders = fin_ref.shape[0]
    edge = cols // holders
    values = jnp.broadcast_to(fin_ref[...], (holders, edge, cols)).reshape(cols, cols)
    block = lax.broadcasted_iota(I32, (cols, cols), 1) // (planes * rows)
    column = lax.broadcasted_iota(I32, (cols, cols), 0)
    values = jnp.where(lax.rem(block, edge) == lax.rem(column, edge), values, 0.0)
    turned = jnp.transpose(values)
    half = cols // 2
    result = turned[:half].reshape(edge, planes * rows, cols).sum(axis=0)
    depth = turned[half:].reshape(edge, planes * rows, cols).sum(axis=0)
    for r in range(rows):
        depth_ref[r : r + 1, :] = depth[r : r + 1]
        for p in range(planes):
            prob_ref[p, r : r + 1, :] = result[p * rows + r : p * rows + r + 1]


def body(ref_feat, src_feat, tile_owner, tile_local, col_shift, w_gates, bias_z, bias_c, w_out):
    n = lax.axis_size("depth")
    rows, feat, cols = ref_feat.shape
    groups = w_gates.shape[2]
    hidden = w_gates.shape[1] // 2
    requests = tile_owner.shape[0]
    cap = max(2, (3 * requests + 2 * n - 1) // (2 * n))
    tiles = (n, 8, cols)
    holders = (cols // 8, 8, cols)
    span = PD * rows * hidden
    anywhere = pl.BlockSpec(memory_space=pl.ANY)
    vmem = pl.BlockSpec(memory_space=pltpu.VMEM)
    shapes = (
        jax.ShapeDtypeStruct((PD, rows, cols), F32),
        jax.ShapeDtypeStruct((rows, cols), F32),
    )
    landed = pl.pallas_call(
        functools.partial(kernel, n, cap),
        out_shape=pltpu.VMEM((holders[0], 1, cols), F32),
        in_specs=[anywhere] * 9,
        out_specs=vmem,
        scratch_shapes=[
            pltpu.VMEM(ref_feat.shape, ref_feat.dtype),
            pltpu.VMEM(src_feat.shape, src_feat.dtype),
            pltpu.VMEM((1, requests), I32),
            pltpu.VMEM((1, requests), I32),
            pltpu.VMEM((1, requests), I32),
            pltpu.VMEM((9, groups, 2 * hidden), w_gates.dtype),
            pltpu.VMEM((1, hidden), F32),
            pltpu.VMEM((1, hidden), F32),
            pltpu.VMEM((1, hidden), F32),
            pltpu.VMEM(ref_feat.shape, F32),
            pltpu.VMEM((n, 1, cols), I32),
            pltpu.VMEM((n, 1, cols), I32),
            pltpu.SMEM((n, 1, cols), I32),
            pltpu.VMEM((1, cols), I32),
            pltpu.SMEM((1, cols), I32),
            pltpu.VMEM((2 * cap, feat, cols), F32),
            pltpu.VMEM((n * cap * groups, cols), jnp.int16),
            pltpu.VMEM((n * cap * groups, cols), jnp.int16),
            pltpu.VMEM((n, cap, cols), F32),
            pltpu.VMEM((n, cap, cols), F32),
            pltpu.VMEM((n * cap, groups, cols), F32),
            pltpu.VMEM((3 * cols, 2 * span), F32),
            pltpu.VMEM((3 * cols, 2 * span), jnp.bfloat16),
            pltpu.VMEM(holders, F32),
            pltpu.VMEM(tiles, F32),
            pltpu.VMEM(holders, F32),
            pltpu.VMEM(tiles, F32),
            pltpu.VMEM(tiles, F32),
            pltpu.VMEM((n, 1, cols), F32),
            pltpu.SemaphoreType.DMA((9,)),
            pltpu.SemaphoreType.DMA((2,)),
            pltpu.SemaphoreType.DMA((6,)),
            pltpu.SemaphoreType.DMA((6,)),
        ],
        compiler_params=pltpu.CompilerParams(
            collective_id=0, has_side_effects=True, vmem_limit_bytes=60 * 1024 * 1024
        ),
        cost_estimate=pl.CostEstimate(
            flops=2 * 144 * 64 * 1024, bytes_accessed=src_feat.size * 2, transcendentals=65536
        ),
    )(
        ref_feat, src_feat, tile_owner.reshape(1, requests), tile_local.reshape(1, requests),
        col_shift.reshape(1, requests), jnp.transpose(w_gates, (0, 2, 1)), bias_z.reshape(1, hidden),
        bias_c.reshape(1, hidden), w_out.reshape(1, hidden),
    )
    return pl.pallas_call(
        hand_over,
        out_shape=shapes,
        in_specs=[vmem],
        out_specs=(vmem, vmem),
    )(landed)


def solution(mesh):
    return jax.shard_map(
        body,
        mesh=mesh,
        in_specs=(
            P("slab", None, None),
            P("depth", None, None),
            P(("depth", "slab"), None),
            P(("depth", "slab")),
            P(("depth", "slab")),
            P(),
            P(),
            P(),
            P(),
        ),
        out_specs=(P("depth", "slab", None), P("slab", None)),
        check_vma=False,
    )
```

```python
import functools

import jax
import jax.numpy as jnp
from jax import lax
from jax.experimental import pallas as pl
from jax.experimental.pallas import tpu as pltpu
from jax.sharding import PartitionSpec as P

VIEWS = 5
PD = 4
MAXSHIFT = 16
MESH = pl.DeviceIdType.MESH
F32 = jnp.float32
I32 = jnp.int32


def kernel(
    n, cap,
    ref_hbm, src_hbm, owner_hbm, local_hbm, shift_hbm, w_hbm, bz_hbm, bc_hbm, wo_hbm,
    fin_recv,
    ref_ref, src, owner_ref, local_ref, shift_ref, w_ref, bz_ref, bc_ref, wo_ref,
    ref_wide, tab_send, tab_recv, tab_s, own_v, own_s, prod, code_send, code_recv,
    scale_send, scale_recv, answers,
    gates_wide, gates, own_send, own_recv, side_send, side_recv, entry, fin_send,
    in_sems, smem_sems, send_sems, recv_sems,
):
    me = lax.axis_index("depth")
    slab = lax.axis_index("slab")
    requests = owner_ref.shape[1]
    rows, feat, cols = ref_ref.shape
    groups = w_ref.shape[1]
    hidden = w_ref.shape[2] // 2
    cpg = feat // groups

    edge = 8
    holders = cols // edge
    once = n <= 16

    def peer(k):
        return lax.rem(me + k, n)

    def far(j):
        step = (j + 1) // 2
        return peer(n // 2 + jnp.where(lax.rem(j, 2) == 1, -step, step))

    pairs = [
        (owner_hbm, owner_ref), (local_hbm, local_ref), (shift_hbm, shift_ref), (ref_hbm, ref_ref),
        (src_hbm, src), (w_hbm, w_ref), (bz_hbm, bz_ref), (bc_hbm, bc_ref), (wo_hbm, wo_ref),
    ]
    loads = [pltpu.make_async_copy(a, b, in_sems.at[i]) for i, (a, b) in enumerate(pairs)]
    for load in loads:
        load.start()
    barrier = pltpu.get_barrier_semaphore()

    def greet(k, carry):
        pl.semaphore_signal(barrier, inc=1, device_id={"depth": peer(k)}, device_id_type=MESH)
        return carry

    def greet_side(k, carry):
        who = {"depth": peer(k), "slab": 1 - slab}
        pl.semaphore_signal(barrier, inc=1, device_id=who, device_id_type=MESH)
        return carry

    lax.fori_loop(1, n, greet, 0, unroll=once)
    lax.fori_loop(0, n, greet_side, 0, unroll=once)

    q_sub = lax.broadcasted_iota(I32, (requests, requests), 0)
    q_lane = lax.broadcasted_iota(I32, (requests, requests), 1)
    diag = q_sub == q_lane
    for load in loads[:3]:
        load.wait()
    owner_row = owner_ref[...]
    owner_col = jnp.sum(
        jnp.where(diag, owner_row, 0).astype(F32), axis=1, keepdims=True
    ).astype(I32)
    local_col = jnp.sum(jnp.where(diag, local_ref[...], 0).astype(F32), axis=1, keepdims=True)
    shift_col = jnp.sum(
        jnp.where(diag, shift_ref[...] + MAXSHIFT, 0).astype(F32), axis=1, keepdims=True
    )
    same = (owner_row == owner_col) & (q_lane < q_sub)
    slot_col = jnp.sum(jnp.where(same, 1.0, 0.0), axis=1, keepdims=True)
    lane = lax.broadcasted_iota(I32, (requests, cols), 1)
    row_col = lax.rem(lax.broadcasted_iota(I32, (requests, cols), 0), rows).astype(F32)
    kind = lane // cap
    value = jnp.where(
        kind == 0, local_col, jnp.where(kind == 1, shift_col, jnp.where(kind == 2, row_col, 0.0))
    )
    value = jnp.where(lax.rem(lane, cap).astype(F32) == slot_col, value, 0.0)
    owner_hot = jnp.where(
        lax.broadcasted_iota(I32, (n, requests), 0) == owner_row, 1.0, 0.0
    )
    table = jnp.dot(
        owner_hot.astype(jnp.bfloat16), value.astype(jnp.bfloat16), preferred_element_type=F32
    ).astype(I32)
    tab_send[:, 0, :] = table
    place_col = owner_col.astype(F32) * cap + slot_col
    wide_diag = lax.broadcasted_iota(I32, (requests, cols), 0) == lane
    own_v[...] = jnp.sum(jnp.where(wide_diag, place_col, 0.0), axis=0, keepdims=True).astype(I32)
    own_copy = pltpu.make_async_copy(own_v, own_s, smem_sems.at[0])
    own_copy.start()

    def push(source, target, who, number):
        return pltpu.make_async_remote_copy(
            src_ref=source, dst_ref=target, send_sem=send_sems.at[number],
            recv_sem=recv_sems.at[number], device_id=who, device_id_type=MESH,
        )

    def drain_part(buffer, count, part, number, sems):
        got = buffer.at[pl.ds(0, count), part]
        pltpu.make_async_copy(got, got, sems.at[number]).wait()

    def drain(buffer, count, number, sems):
        part = buffer.at[pl.ds(0, count)]
        pltpu.make_async_copy(part, part, sems.at[number]).wait()

    pl.semaphore_wait(barrier, 2 * n - 1)

    def send_table(k, carry):
        to = far(k)
        push(tab_send.at[to], tab_recv.at[me], {"depth": to}, 0).start()
        return carry

    lax.fori_loop(0, n - 1, send_table, 0, unroll=once)
    tab_recv[me] = tab_send[me]
    for load in loads[3:5]:
        load.wait()

    def regroup(at):
        return [prod[at, pl.ds(c, groups, stride=cpg), :] for c in range(cpg)]

    for r in range(rows):
        prod[r] = ref_ref[r].astype(F32)
    for r in range(rows):
        ref_wide[r] = jnp.concatenate(regroup(r), axis=0)
    drain(tab_recv, n - 1, 0, recv_sems)
    tab_copy = pltpu.make_async_copy(tab_recv, tab_s, smem_sems.at[1])
    tab_copy.start()
    tab_copy.wait()

    position = lax.broadcasted_iota(I32, (groups, cols), 1)

    top_code = 32767.0

    def correlate(whos):
        slots = [(who, s) for who in whos for s in range(cap)]
        tiles, shifts, picked = [], [], []
        for who, s in slots:
            tiles.append(jnp.clip(tab_s[who, 0, s], 0, src.shape[0] - 1))
            shifts.append(jnp.clip(tab_s[who, 0, cap + s], 0, 2 * MAXSHIFT) - MAXSHIFT)
            picked.append(jnp.clip(tab_s[who, 0, 2 * cap + s], 0, rows - 1))
        for i, tile in enumerate(tiles):
            prod[i] = src[tile].astype(F32)
        wide = [jnp.concatenate(regroup(i), axis=0) for i in range(len(slots))]
        moved = [pltpu.roll(x, lax.rem(y + cols, cols), 1) for x, y in zip(wide, shifts)]
        totals = []
        for i in range(len(slots)):
            terms = moved[i] * ref_wide[picked[i]]
            total = terms[0:groups]
            for c in range(1, cpg):
                total = total + terms[c * groups : (c + 1) * groups]
            source_col = position - shifts[i]
            inside = (source_col >= 0) & (source_col < cols)
            totals.append(jnp.where(inside, total, 0.0))
        return [totals[i * cap : (i + 1) * cap] for i in range(len(whos))]

    code_rows = cap * groups

    def dispatch(to, totals):
        codes = []
        for s, total in enumerate(totals):
            largest = jnp.maximum(jnp.max(jnp.abs(total), axis=0, keepdims=True), 1e-30)
            codes.append(jnp.round(total * (top_code / largest)).astype(I32))
            scale_send[to, s : s + 1, :] = largest * (1.0 / (top_code * VIEWS * cpg))
        at = pl.ds(pl.multiple_of(to * code_rows, code_rows), code_rows)
        code_send[at, :] = jnp.concatenate(codes, axis=0).astype(jnp.int16)
        home = pl.ds(pl.multiple_of(me * code_rows, code_rows), code_rows)
        push(code_send.at[at], code_recv.at[home], {"depth": to}, 1).start()
        push(scale_send.at[to], scale_recv.at[me], {"depth": to}, 5).start()

    def answer(k, carry):
        pair = [far(2 * k), far(2 * k + 1)]
        for to, totals in zip(pair, correlate(pair)):
            dispatch(to, totals)
        return carry

    lax.fori_loop(0, (n - 1) // 2, answer, 0)
    last = far(n - 2)
    for_last, for_me = correlate([last, me])
    dispatch(last, for_last)
    for s in range(cap):
        answers[me * cap + s] = for_me[s] * (1.0 / (VIEWS * cpg))
    for load in loads[5:]:
        load.wait()
    taps = [w_ref[t].astype(F32) for t in range(9)]
    span = PD * rows * hidden
    plane_of = lax.broadcasted_iota(I32, (groups, span), 1) // (rows * hidden)

    def fill(at, pieces):
        for kind in range(2):
            units = slice(kind * hidden, (kind + 1) * hidden)
            part = jnp.concatenate([x[:, units] for x in pieces] * PD, axis=1)
            for p in range(PD):
                gates_wide[pl.ds(at(p), groups), pl.ds(kind * span, span)] = jnp.where(
                    plane_of == p, part, 0.0
                )

    own_rows = PD * rows * groups
    for b in range(3):
        for r in range(rows):
            fill(
                lambda p: b * cols + (p * rows + r) * groups,
                [taps[(r - to + 1) * 3 + b] for to in range(rows)],
            )
        pieces = [jnp.zeros((groups, 2 * hidden), F32) for _ in range(rows)]
        pieces[0] = pieces[0] + jnp.where(slab == 1, taps[b], 0.0)
        pieces[-1] = pieces[-1] + jnp.where(slab == 0, taps[6 + b], 0.0)
        fill(lambda p: b * cols + own_rows + p * groups, pieces)
        rest = own_rows + PD * groups
        gates_wide[pl.ds(b * cols + rest, cols - rest), :] = jnp.zeros((cols - rest, 2 * span), F32)
    gates[...] = gates_wide[...].astype(jnp.bfloat16)
    bias_z = jnp.concatenate([bz_ref[...]] * (PD * rows), axis=1)
    bias_c = jnp.concatenate([bc_ref[...]] * (PD * rows), axis=1)
    h_eye = lax.broadcasted_iota(I32, (hidden, hidden), 0) == lax.broadcasted_iota(
        I32, (hidden, hidden), 1
    )
    out_col = jnp.sum(jnp.where(h_eye, wo_ref[...], 0.0), axis=1, keepdims=True)
    out_col = jnp.concatenate([out_col] * (PD * rows), axis=0)
    unit_block = lax.broadcasted_iota(I32, (span, cols), 0) // hidden
    lane_block = lax.rem(lax.broadcasted_iota(I32, (span, cols), 1), PD * rows)
    out_wide = jnp.where(unit_block == lane_block, out_col, 0.0)
    out_high = out_wide.astype(jnp.bfloat16)
    out_low = (out_wide - out_high.astype(F32)).astype(jnp.bfloat16)
    own_copy.wait()
    drain(code_recv, code_rows * (n - 1), 1, recv_sems)
    drain(scale_recv, n - 1, 5, recv_sems)

    def decode(k, carry):
        source = peer(k)
        at = pl.ds(pl.multiple_of(source * code_rows, code_rows), code_rows)
        values = code_recv[at, :].astype(I32).astype(F32)
        for s in range(cap):
            part = values[s * groups : (s + 1) * groups]
            answers[source * cap + s] = part * scale_recv[source, s : s + 1, :]
        return carry

    lax.fori_loop(1, n, decode, 0, unroll=once)
    cost = {}
    for p in range(PD):
        for r in range(rows):
            total = None
            for v in range(VIEWS):
                place = jnp.clip(own_s[0, (p * VIEWS + v) * rows + r], 0, n * cap - 1)
                term = answers[place]
                total = term if total is None else total + term
            cost[p, r] = total

    in_block = lax.rem(position, edge)

    def turned(x, by):
        moved = pltpu.roll(x, by % cols, 1)
        return jnp.where((position >= by) & (position < cols + by), moved, 0.0)

    blocks = [cost[p, r] for p in range(PD) for r in range(rows)]
    near = [jnp.where(slab == 0, cost[p, rows - 1], cost[p, 0]) for p in range(PD)]
    side = [jnp.where(in_block < 2, x, turned(x, 3)) for x in near]
    side += [jnp.where(in_block < 2, turned(x, -2), turned(x, -6)) for x in near]
    side += [turned(x, -4) for x in near] + [turned(x, -6) for x in near]
    side = jnp.concatenate(side, axis=0)
    side_send[...] = jnp.transpose(side).reshape(holders, edge, cols)
    own_part, side_part = pl.ds(0, 5), pl.ds(0, 3)

    def send_side(k, carry):
        to = far(k) if n == holders else k
        who = {"depth": to, "slab": 1 - slab}
        push(side_send.at[to, side_part], side_recv.at[me, side_part], who, 3).start()
        return carry

    own = [jnp.where(in_block < 4, x, turned(x, 5)) for x in blocks]
    own = jnp.concatenate(own + [turned(x, -4) for x in blocks], axis=0)
    own_send[...] = jnp.transpose(own).reshape(holders, edge, cols)

    def send_own(k, carry):
        to = far(k) if n == holders else k

        def go():
            push(
                own_send.at[to, own_part], own_recv.at[me, own_part], {"depth": to}, 2
            ).start()

        go() if n == holders else pl.when(to != me)(go)
        return carry

    if n == holders:
        def send_both(k, carry):
            send_own(k, carry)
            return send_side(k, carry)

        lax.fori_loop(0, n - 1, send_both, 0, unroll=once)
        send_side_me = {"depth": me, "slab": 1 - slab}
        push(side_send.at[me, side_part], side_recv.at[me, side_part], send_side_me, 3).start()
    else:
        lax.fori_loop(0, holders, send_own, 0)
        lax.fori_loop(0, holders, send_side, 0)

    def hold():
        own_recv[me] = own_send[me]
        drain_part(own_recv, n - 1, own_part, 2, recv_sems)
        drain_part(side_recv, n, side_part, 3, recv_sems)
        count = n * edge
        here = own_recv[...].reshape(count, cols)
        beside = side_recv[...].reshape(count, cols)
        lane = lax.broadcasted_iota(I32, (count, cols), 1)
        place = lax.rem(lax.broadcasted_iota(I32, (count, cols), 0), edge)
        lower = lane < cols // 2

        def down(x, by):
            return pltpu.roll(x, by % count, 0)

        here_2 = pltpu.roll(here, cols // 2, 1)
        quarter = [pltpu.roll(beside, (64 - 32 * q) % cols, 1) if q != 2 else beside for q in range(4)]
        main_1 = jnp.where(place < 4, here, down(here_2, 4))
        main_2 = quarter[0]
        for q in range(1, 4):
            main_2 = jnp.where(place >= 2 * q, down(quarter[q], 2 * q), main_2)
        main = jnp.where(lower, main_1, main_2)
        first = jnp.where(lower, down(here, -4), down(quarter[0], -2))
        final = jnp.where(lower, down(here_2, 3), down(quarter[1], 5))
        before = jnp.where(place == 0, first, down(main, 1))
        after = jnp.where(place == edge - 1, final, down(main, -1))
        live = lane < cols // 2 + PD * groups
        before, main, after = [jnp.where(live, x, 0.0) for x in (before, main, after)]
        window = jnp.concatenate([before, main, after], axis=1)
        high = window.astype(jnp.bfloat16)
        low = (window - high.astype(F32)).astype(jnp.bfloat16)
        both = jnp.dot(
            jnp.concatenate([high, low], axis=0), gates[...], preferred_element_type=F32
        )
        preact = both[:count] + both[count:]
        retain = jax.nn.sigmoid(preact[:, :span] + bias_z)
        fresh = (1.0 - retain) * jnp.tanh(preact[:, span:] + bias_c)

        def planes(x):
            pair = [x[:, :cols], x[:, cols:]]
            return [pair[0], pltpu.roll(pair[0], cols // 2, 1), pair[1], pltpu.roll(pair[1], cols // 2, 1)]

        keep, new = planes(retain), planes(fresh)
        decay, offset = [keep[0]], [new[0]]
        for p in range(1, PD):
            decay.append(keep[p] * decay[-1])
            offset.append(keep[p] * offset[-1] + new[p])
        if once:
            state, entries = jnp.zeros((edge, cols), F32), []
            for i in range(n):
                entries.append(state)
                at = slice(i * edge, (i + 1) * edge)
                state = decay[-1][at] * state + offset[-1][at]
            start = jnp.concatenate(entries, axis=0)
        else:
            own_recv[...] = decay[-1].reshape(n, edge, cols)
            side_recv[...] = offset[-1].reshape(n, edge, cols)

            def compose(i, state):
                entry[i] = state
                return own_recv[i] * state + side_recv[i]

            lax.fori_loop(0, n, compose, jnp.zeros((edge, cols), F32))
            start = entry[...].reshape(count, cols)
        states = [decay[p] * start + offset[p] for p in range(PD)]
        states = jnp.concatenate(
            [
                jnp.where(lower, states[p], pltpu.roll(states[p + 1], cols // 2, 1))
                for p in range(0, PD, 2)
            ],
            axis=1,
        )
        high = states.astype(jnp.bfloat16)
        low = (states - high.astype(F32)).astype(jnp.bfloat16)
        scores = jnp.dot(low, out_high, preferred_element_type=F32) + jnp.dot(
            high, out_low, preferred_element_type=F32
        )
        scores = scores + jnp.dot(high, out_high, preferred_element_type=F32)
        scores = scores.reshape(n, edge, cols)

        def over_planes(x, combine):
            x = combine(x, pltpu.roll(x, rows, 1))
            return combine(x, pltpu.roll(x, 2 * rows, 1))

        highest = over_planes(jnp.max(scores, axis=0), jnp.maximum)
        weights = jnp.exp(scores - highest[None])
        total = over_planes(jnp.sum(weights, axis=0), jnp.add)
        shape = (n, edge, cols)
        plane = lax.rem(lax.broadcasted_iota(I32, shape, 2), PD * rows) // rows
        plane = (plane + PD * lax.broadcasted_iota(I32, shape, 0)).astype(F32)
        value = 1.0 / (0.1 + 0.9 * plane / (PD * n - 1))
        depth = over_planes(jnp.sum(weights * value, axis=0), jnp.add) / total
        block = lax.broadcasted_iota(I32, shape, 2) // (PD * rows)
        column = lax.broadcasted_iota(I32, shape, 1)
        chosen = jnp.where(block == column, weights / total[None], 0.0)
        chosen = jnp.where(block == column + edge, depth[None], chosen)
        fin_send[...] = jnp.sum(chosen, axis=1, keepdims=True)
        fin_own = pltpu.make_async_copy(fin_send.at[me], fin_recv.at[me], smem_sems.at[1])
        fin_own.start()

        def send_fin(k, carry):
            to = far(k)
            push(fin_send.at[to], fin_recv.at[me], {"depth": to}, 4).start()
            return carry

        lax.fori_loop(0, n - 1, send_fin, 0, unroll=once)
        fin_own.wait()
        drain(fin_recv, holders - 1, 4, recv_sems)

    hold() if n == holders else pl.when(me < holders)(hold)
    if n != holders:
        @pl.when(me >= holders)
        def _():
            drain(fin_recv, holders, 4, recv_sems)

    drain(tab_send, n - 1, 0, send_sems)
    drain(code_send, code_rows * (n - 1), 1, send_sems)
    drain(scale_send, n - 1, 5, send_sems)
    drain_part(side_send, holders, side_part, 3, send_sems)
    if n == holders:
        drain_part(own_send, n - 1, own_part, 2, send_sems)
        drain(fin_send, n - 1, 4, send_sems)
    else:
        @pl.when(me < holders)
        def _():
            drain_part(own_send, holders - 1, own_part, 2, send_sems)
            drain(fin_send, n - 1, 4, send_sems)

        @pl.when(me >= holders)
        def _():
            drain_part(own_send, holders, own_part, 2, send_sems)


def hand_over(fin_ref, prob_ref, depth_ref):
    planes, rows, cols = prob_ref.shape
    holders = fin_ref.shape[0]
    edge = cols // holders
    values = jnp.broadcast_to(fin_ref[...], (holders, edge, cols)).reshape(cols, cols)
    block = lax.broadcasted_iota(I32, (cols, cols), 1) // (planes * rows)
    column = lax.broadcasted_iota(I32, (cols, cols), 0)
    values = jnp.where(lax.rem(block, edge) == lax.rem(column, edge), values, 0.0)
    turned = jnp.transpose(values)
    half = cols // 2
    result = turned[:half].reshape(edge, planes * rows, cols).sum(axis=0)
    depth = turned[half:].reshape(edge, planes * rows, cols).sum(axis=0)
    for r in range(rows):
        depth_ref[r : r + 1, :] = depth[r : r + 1]
        for p in range(planes):
            prob_ref[p, r : r + 1, :] = result[p * rows + r : p * rows + r + 1]


def body(ref_feat, src_feat, tile_owner, tile_local, col_shift, w_gates, bias_z, bias_c, w_out):
    n = lax.axis_size("depth")
    rows, feat, cols = ref_feat.shape
    groups = w_gates.shape[2]
    hidden = w_gates.shape[1] // 2
    requests = tile_owner.shape[0]
    cap = max(2, (3 * requests + 2 * n - 1) // (2 * n))
    tiles = (n, 8, cols)
    holders = (cols // 8, 8, cols)
    span = PD * rows * hidden
    anywhere = pl.BlockSpec(memory_space=pl.ANY)
    vmem = pl.BlockSpec(memory_space=pltpu.VMEM)
    shapes = (
        jax.ShapeDtypeStruct((PD, rows, cols), F32),
        jax.ShapeDtypeStruct((rows, cols), F32),
    )
    landed = pl.pallas_call(
        functools.partial(kernel, n, cap),
        out_shape=pltpu.VMEM((holders[0], 1, cols), F32),
        in_specs=[anywhere] * 9,
        out_specs=vmem,
        scratch_shapes=[
            pltpu.VMEM(ref_feat.shape, ref_feat.dtype),
            pltpu.VMEM(src_feat.shape, src_feat.dtype),
            pltpu.VMEM((1, requests), I32),
            pltpu.VMEM((1, requests), I32),
            pltpu.VMEM((1, requests), I32),
            pltpu.VMEM((9, groups, 2 * hidden), w_gates.dtype),
            pltpu.VMEM((1, hidden), F32),
            pltpu.VMEM((1, hidden), F32),
            pltpu.VMEM((1, hidden), F32),
            pltpu.VMEM(ref_feat.shape, F32),
            pltpu.VMEM((n, 1, cols), I32),
            pltpu.VMEM((n, 1, cols), I32),
            pltpu.SMEM((n, 1, cols), I32),
            pltpu.VMEM((1, cols), I32),
            pltpu.SMEM((1, cols), I32),
            pltpu.VMEM((2 * cap, feat, cols), F32),
            pltpu.VMEM((n * cap * groups, cols), jnp.int16),
            pltpu.VMEM((n * cap * groups, cols), jnp.int16),
            pltpu.VMEM((n, cap, cols), F32),
            pltpu.VMEM((n, cap, cols), F32),
            pltpu.VMEM((n * cap, groups, cols), F32),
            pltpu.VMEM((3 * cols, 2 * span), F32),
            pltpu.VMEM((3 * cols, 2 * span), jnp.bfloat16),
            pltpu.VMEM(holders, F32),
            pltpu.VMEM(tiles, F32),
            pltpu.VMEM(holders, F32),
            pltpu.VMEM(tiles, F32),
            pltpu.VMEM(tiles, F32),
            pltpu.VMEM((n, 1, cols), F32),
            pltpu.SemaphoreType.DMA((9,)),
            pltpu.SemaphoreType.DMA((2,)),
            pltpu.SemaphoreType.DMA((6,)),
            pltpu.SemaphoreType.DMA((6,)),
        ],
        compiler_params=pltpu.CompilerParams(
            collective_id=0, has_side_effects=True, vmem_limit_bytes=60 * 1024 * 1024
        ),
        cost_estimate=pl.CostEstimate(
            flops=2 * 144 * 64 * 1024, bytes_accessed=src_feat.size * 2, transcendentals=65536
        ),
    )(
        ref_feat, src_feat, tile_owner.reshape(1, requests), tile_local.reshape(1, requests),
        col_shift.reshape(1, requests), jnp.transpose(w_gates, (0, 2, 1)), bias_z.reshape(1, hidden),
        bias_c.reshape(1, hidden), w_out.reshape(1, hidden),
    )
    return pl.pallas_call(
        hand_over,
        out_shape=shapes,
        in_specs=[vmem],
        out_specs=(vmem, vmem),
        compiler_params=pltpu.CompilerParams(vmem_limit_bytes=4 * 1024 * 1024),
    )(landed)


def solution(mesh):
    return jax.shard_map(
        body,
        mesh=mesh,
        in_specs=(
            P("slab", None, None),
            P("depth", None, None),
            P(("depth", "slab"), None),
            P(("depth", "slab")),
            P(("depth", "slab")),
            P(),
            P(),
            P(),
            P(),
        ),
        out_specs=(P("depth", "slab", None), P("slab", None)),
        check_vma=False,
    )
```
